512 devices in a mesh: expert: 32 (over x, y, core), tensor: 16 (over z).
Axes of the slice: x: 4, y: 4, z: 16, core: 2. Of those that a mesh axis runs over, the one named last changes fastest.
Arguments:
- picked_rows: bfloat16 [32, 256, 6144], P('expert', None, 'tensor'), may hold values from -6 to 6
- w_gate: bfloat16 [32, 6144, 1536], P('expert', 'tensor'), may hold values from -0.078125 to 0.078125
- w_up: bfloat16 [32, 6144, 1536], P('expert', 'tensor'), may hold values from -0.078125 to 0.078125
- w_down: bfloat16 [32, 1536, 6144], P('expert', None, 'tensor'), may hold values from -0.15625 to 0.15625
- combine_gate: float32 [32, 256], P('expert'), may hold values from 0.3 to 3
- pick_owner: int32 [32, 256], replicated, may hold values from 0 to 31, as said below
- pick_row: int32 [32, 256], replicated, may hold values from 0 to 767, as said below
- residual_in: bfloat16 [24576, 6144], P('expert', 'tensor'), may hold values from -60 to 60
- norm_gain: float32 [6144], P('tensor'), may hold values from 0.5 to 2
- projection: bfloat16 [6144, 6144], P('expert', 'tensor'), may hold values from -0.078125 to 0.078125
Outputs:
- projected: bfloat16 [24576, 6144], P('expert', 'tensor')
The draws below stay inside these ranges and needn't reach their ends.
Inputs may be any that keep to these rules, and one draw needn't show every extreme that they name: `pick_owner`: for every expert, at most 24 of its picks have one owner group, and one owner group gets exactly 24 picks from every expert. The picks of one expert are distinct tokens. `pick_row`: together with pick_owner it names a token; no expert names a token twice.
All inputs are finite; a program needn't handle non-finite values.
Results may differ from the reference program's by a relative error of at most 0.0051.
Values may be sent and summed in bfloat16 or wider, within the bound.
No kernel may reach another device: no remote copies, remote signals or barrier semaphores. Data moves between devices by JAX's collectives and lax.ppermute only.
A program may use at most 64 MiB of HBM per device.

```python
import math
import jax
import jax.numpy as jnp
from jax import lax

D = 6144
FF = 1536
CAP = 256
EXPERTS = 32
TOK_GROUP = 768
TOKENS = 24576
MOST = 24
QKV = 6144


def choose_picks(key):
    hot_key, expert_keys = jax.random.split(key)
    hot_owner = jax.random.randint(hot_key, (), 0, EXPERTS)
    slot_owner = jnp.arange(EXPERTS * MOST, dtype=jnp.int32) // MOST

    def one_expert(expert_key):
        cand_key, score_key = jax.random.split(expert_key)
        owner_keys = jax.random.split(cand_key, EXPERTS)
        candidates = jax.vmap(lambda owner_key: jax.random.permutation(owner_key, TOK_GROUP)[:MOST])(owner_keys)
        rank_order = jax.random.permutation(score_key, EXPERTS * MOST)
        scores = rank_order + jnp.where(slot_owner == hot_owner, EXPERTS * MOST, 0)
        scores_top, chosen = lax.top_k(scores, CAP)
        return (slot_owner[chosen], candidates.reshape(-1)[chosen])
    owners, rows_all = jax.vmap(one_expert)(jax.random.split(expert_keys, EXPERTS))
    return (owners.astype(jnp.int32), rows_all.astype(jnp.int32))


def draw_pick_owner(key, part):
    owners, rows_all = choose_picks(key)
    return owners


def draw_pick_row(key, part):
    owners, rows_all = choose_picks(key)
    return rows_all


def draw_residual_in(key, part):
    key = jax.random.fold_in(key, 7)
    base_key, row_key, col_key = jax.random.split(key, 3)
    col_ramp = 3.0 ** (jnp.arange(D, dtype=jnp.float32) / D - 0.5)
    row_scale = jnp.exp(jax.random.uniform(row_key, (TOKENS, 1), jnp.float32, -1.15, 1.15))
    col_scale = jnp.exp(jax.random.uniform(col_key, (1, D), jnp.float32, -0.6, 0.6)) * col_ramp[None, :]
    values_base = jnp.clip(jax.random.normal(base_key, (TOKENS, D), jnp.float32), -4.0, 4.0)
    values = jnp.clip(values_base * row_scale * col_scale, -60.0, 60.0)
    return values.astype(jnp.bfloat16)


def levels(rng, dims, cuts, low, largest):
    factor_of = 1.0
    for position, shards_of in cuts:
        steps = jax.random.uniform(jax.random.fold_in(jax.random.fold_in(rng, 6), position), (shards_of,), jnp.float32, low / len(cuts), largest / len(cuts))
        factor_of = factor_of * jnp.repeat(jnp.exp(steps), dims[position] // shards_of).reshape((-1,) + (1,) * (len(dims) - 1 - position))
    return factor_of


def noise(rng, extent, scale, most, pieces=(), kind=jnp.bfloat16):
    drawn = jax.random.normal(rng, extent, jnp.float32) * scale
    if len(pieces) > 0:
        drawn = levels(rng, extent, pieces, -0.22, 0.18) * drawn
    return jnp.clip(drawn, min=-most, max=most).astype(kind)


def setup_inputs(seed: int = 0) -> dict:
    key_of = jax.random.split(jax.random.key(seed), 11)
    picked_rows = noise(key_of[0], (EXPERTS, CAP, D), 1.0, 6.0, ((0, 32), (2, 16)))
    w_gate = noise(key_of[1], (EXPERTS, D, FF), D ** -0.5, 0.078125, ((0, 32), (1, 16)))
    w_up = noise(key_of[2], (EXPERTS, D, FF), D ** -0.5, 0.078125, ((0, 32), (1, 16)))
    w_down = noise(key_of[3], (EXPERTS, FF, D), FF ** -0.5, 0.15625, ((0, 32), (2, 16)))
    combine_gate = jnp.clip(jnp.exp(math.log(3.0) - 2.3025851 * jax.random.uniform(key_of[4], (EXPERTS, CAP), jnp.float32) ** levels(key_of[4], (EXPERTS, CAP), ((0, 32),), -0.2, 0.2)), 0.3, 3.0)
    pick_owner = draw_pick_owner(jax.random.fold_in(key_of[10], 71), 0)
    pick_row = draw_pick_row(jax.random.fold_in(key_of[10], 71), 0)
    residual_in = draw_residual_in(jax.random.fold_in(key_of[10], 71), 0)
    norm_gain = jnp.clip(jnp.exp(math.log(2.0) - 1.3862944 * jax.random.uniform(key_of[8], (D,), jnp.float32) ** levels(key_of[8], (D,), ((0, 16),), -0.2, 0.2)), 0.5, 2.0)
    projection = noise(key_of[9], (D, QKV), D ** -0.5, 0.078125, ((0, 32), (1, 16)))
    return {"picked_rows": picked_rows, "w_gate": w_gate, "w_up": w_up, "w_down": w_down, "combine_gate": combine_gate, "pick_owner": pick_owner, "pick_row": pick_row, "residual_in": residual_in, "norm_gain": norm_gain, "projection": projection}


def expert_rows(operands):
    my_rows, gate_mat, up_mat, down_mat, weights = operands
    gate_pre = jnp.dot(my_rows, gate_mat, preferred_element_type=jnp.float32)
    up_pre = jnp.dot(my_rows, up_mat, preferred_element_type=jnp.float32)
    hidden = (jax.nn.silu(gate_pre) * up_pre).astype(jnp.bfloat16)
    output = jnp.dot(hidden, down_mat, preferred_element_type=jnp.float32)
    return (weights[:, None] * output).astype(jnp.bfloat16)

def reference(picked_rows, w_gate, w_up, w_down, combine_gate, pick_owner, pick_row, residual_in, norm_gain, projection):
    weighted = lax.map(expert_rows, (picked_rows, w_gate, w_up, w_down, combine_gate))
    target = (pick_owner * TOK_GROUP + pick_row).reshape(-1).astype(jnp.int32)
    moe = jnp.zeros((TOKENS, D), jnp.float32).at[target].add(weighted.reshape(-1, D).astype(jnp.float32))
    mixed = residual_in.astype(jnp.float32) + moe
    inverse_rms = lax.rsqrt(lax.optimization_barrier(jnp.mean(mixed * mixed, axis=1, keepdims=True)) + 1e-05)
    normed = (mixed * inverse_rms * norm_gain[None, :]).astype(jnp.bfloat16)
    return jnp.dot(normed, projection, preferred_element_type=jnp.float32).astype(jnp.bfloat16)
```

```python
import jax
import jax.numpy as jnp
from jax import lax
from jax.experimental import pallas as pl
from jax.experimental.pallas import tpu as pltpu
from jax.sharding import PartitionSpec as P

D = 6144
PIECE_ROWS = 16
PIECE_COLS = 512
VMEM_BYTES = 48 * 1024 * 1024


def piece_places(capacity, ff):
    return [(r, c) for r in range(0, capacity, PIECE_ROWS) for c in range(0, ff, PIECE_COLS)]


def gate_up_kernel(rows_ref, gate_ref, up_ref, *out_refs):
    capacity, ff = rows_ref.shape[0], gate_ref.shape[1]
    n_row = capacity // PIECE_ROWS
    n_col = ff // PIECE_COLS
    rows = rows_ref[...]
    for half, weights in enumerate((gate_ref, up_ref)):
        for c in range(n_col):
            part = jnp.dot(
                rows,
                weights[:, c * PIECE_COLS : (c + 1) * PIECE_COLS],
                preferred_element_type=jnp.float32,
            )
            for r in range(n_row):
                out_refs[(half * n_row + r) * n_col + c][...] = part[
                    r * PIECE_ROWS : (r + 1) * PIECE_ROWS
                ]


def gate_up(rows, gate_mat, up_mat):
    n_pieces = 2 * len(piece_places(rows.shape[0], gate_mat.shape[1]))
    return pl.pallas_call(
        gate_up_kernel,
        out_shape=[jax.ShapeDtypeStruct((PIECE_ROWS, PIECE_COLS), jnp.float32)] * n_pieces,
        in_specs=[pl.BlockSpec(memory_space=pltpu.VMEM)] * 3,
        out_specs=[pl.BlockSpec(memory_space=pltpu.VMEM)] * n_pieces,
        compiler_params=pltpu.CompilerParams(vmem_limit_bytes=VMEM_BYTES),
        name="gate_up",
    )(rows, gate_mat, up_mat)


def tail_kernel(down_ref, combine_ref, slot_ref, *refs):
    out_ref, hidden_ref = refs[-2:]
    pieces = refs[:-2]
    capacity, ff = hidden_ref.shape
    half = len(pieces) // 2
    for k, (r, c) in enumerate(piece_places(capacity, ff)):
        gate = pieces[k][...]
        up = pieces[half + k][...]
        hidden_ref[r : r + PIECE_ROWS, c : c + PIECE_COLS] = (gate / (1.0 + jnp.exp(-gate)) * up).astype(
            jnp.bfloat16
        )
    expert_out = jnp.dot(hidden_ref[...], down_ref[...], preferred_element_type=jnp.float32)
    weighted = (combine_ref[...] * expert_out).astype(jnp.bfloat16)
    slots = out_ref.shape[0]
    slot_ids = lax.broadcasted_iota(jnp.int32, (slots, capacity), 0)
    table = jnp.where(slot_ref[...] == slot_ids, 1.0, 0.0).astype(jnp.bfloat16)
    out_ref[...] = jnp.dot(table, weighted, preferred_element_type=jnp.float32).astype(jnp.bfloat16)


def expert_tail(pieces, down_mat, combine, slot, slots):
    ff, width = down_mat.shape
    capacity = combine.shape[0]
    return pl.pallas_call(
        tail_kernel,
        out_shape=jax.ShapeDtypeStruct((slots, width), jnp.bfloat16),
        in_specs=[pl.BlockSpec(memory_space=pltpu.VMEM)] * (3 + len(pieces)),
        out_specs=pl.BlockSpec(memory_space=pltpu.VMEM),
        scratch_shapes=[pltpu.VMEM((capacity, ff), jnp.bfloat16)],
        compiler_params=pltpu.CompilerParams(vmem_limit_bytes=VMEM_BYTES),
        name="expert_tail",
    )(down_mat, combine[:, None], slot[None, :], *pieces)


def shards(
    picked_rows,
    w_gate,
    w_up,
    w_down,
    combine_gate,
    pick_owner,
    pick_row,
    residual_in,
    norm_gain,
    projection,
):
    my_rows = picked_rows[0]
    capacity = my_rows.shape[0]
    n_groups = pick_owner.shape[0]
    slot_most = max(3 * capacity // n_groups, 2)
    tok_group, width = residual_in.shape
    my_index = lax.axis_index("expert")

    full_projection = lax.all_gather(projection, "expert", axis=0, tiled=True)

    parts = gate_up(my_rows, w_gate[0], w_up[0])

    my_owner = lax.dynamic_index_in_dim(pick_owner, my_index, 0, keepdims=False)
    pick_ids = jnp.arange(capacity, dtype=jnp.int32)
    same_earlier = (my_owner[:, None] == my_owner[None, :]) & (pick_ids[:, None] < pick_ids[None, :])
    my_position = jnp.sum(same_earlier.astype(jnp.int32), axis=0)
    my_slot = my_owner * slot_most + my_position

    mine = pick_owner == my_index
    before = (pick_ids[:, None] < pick_ids[None, :]).astype(jnp.bfloat16)
    position = jnp.dot(
        mine.astype(jnp.bfloat16), before, preferred_element_type=jnp.float32
    ).astype(jnp.int32)
    slot_range = jnp.arange(slot_most, dtype=jnp.int32)
    matches = mine[:, None, :] & (position[:, None, :] == slot_range[None, :, None])
    row_of = jnp.sum(jnp.where(matches, pick_row[:, None, :] + 1, 0), axis=2) - 1
    token_ids = jnp.arange(tok_group, dtype=jnp.int32)
    recv_table = (row_of.reshape(-1)[None, :] == token_ids[:, None]).astype(jnp.bfloat16)

    sums = lax.psum(tuple(parts), "tensor")
    outgoing = expert_tail(sums, w_down[0], combine_gate[0], my_slot, n_groups * slot_most)
    outgoing = outgoing.reshape(n_groups, slot_most, width)
    received = lax.all_to_all(outgoing, "expert", split_axis=0, concat_axis=0, tiled=True)
    moe = jnp.dot(
        recv_table,
        received.reshape(n_groups * slot_most, width),
        preferred_element_type=jnp.float32,
    )
    mixed = residual_in.astype(jnp.float32) + moe
    gained = (mixed * norm_gain[None, :]).astype(jnp.bfloat16)
    full_gained = lax.all_gather(gained, "tensor", axis=1, tiled=True)
    square_total = lax.psum(jnp.sum(mixed * mixed, axis=1), "tensor")
    inverse_rms = lax.rsqrt(square_total / D + 1e-05)
    projected = jnp.dot(full_gained, full_projection, preferred_element_type=jnp.float32)
    return (projected * inverse_rms[:, None]).astype(jnp.bfloat16)


def solution(mesh):
    return jax.shard_map(
        shards,
        mesh=mesh,
        in_specs=(
            P("expert", None, "tensor"),
            P("expert", "tensor", None),
            P("expert", "tensor", None),
            P("expert", None, "tensor"),
            P("expert", None),
            P(),
            P(),
            P("expert", "tensor"),
            P("tensor"),
            P("expert", "tensor"),
        ),
        out_specs=P("expert", "tensor"),
        check_vma=False,
    )
```

```python
import jax
import jax.numpy as jnp
from jax import lax
from jax.experimental import pallas as pl
from jax.experimental.pallas import tpu as pltpu
from jax.sharding import PartitionSpec as P

D = 6144
PIECE_ROWS = 16
PIECE_COLS = 768
VMEM_BYTES = 48 * 1024 * 1024
TAIL_VMEM_BYTES = 63 * 1024 * 1024


def piece_places(capacity, ff):
    return [(r, c) for r in range(0, capacity, PIECE_ROWS) for c in range(0, ff, PIECE_COLS)]


def gate_up_kernel(rows_ref, gate_ref, up_ref, *refs):
    spare_ref, parts_ref, spare_part_ref, sems = refs[-4:]
    out_refs = refs[:-4]
    capacity, ff = rows_ref.shape[0], gate_ref.shape[1]
    places = piece_places(capacity, ff)
    spare_part_ref[...] = jnp.zeros_like(spare_part_ref)
    copies = [pltpu.make_async_copy(spare_part_ref, spare_ref, sems.at[len(out_refs)])]
    copies[0].start()
    rows = rows_ref[...]
    for half, weights in enumerate((gate_ref, up_ref)):
        parts_ref[half] = jnp.dot(rows, weights[...], preferred_element_type=jnp.float32)
        for k, (r, c) in enumerate(places):
            n = half * len(places) + k
            copy = pltpu.make_async_copy(
                parts_ref.at[half, r : r + PIECE_ROWS, c : c + PIECE_COLS], out_refs[n], sems.at[n]
            )
            copy.start()
            copies.append(copy)
    for copy in copies:
        copy.wait()


def gate_up(rows, gate_mat, up_mat):
    capacity, ff = rows.shape[0], gate_mat.shape[1]
    n_pieces = 2 * len(piece_places(capacity, ff))
    return pl.pallas_call(
        gate_up_kernel,
        out_shape=[pltpu.HBM((PIECE_ROWS, PIECE_COLS), jnp.float32)] * n_pieces
        + [pltpu.HBM((8, 128), jnp.float32)],
        in_specs=[pl.BlockSpec(memory_space=pltpu.VMEM)] * 3,
        out_specs=[pl.BlockSpec(memory_space=pltpu.HBM)] * (n_pieces + 1),
        scratch_shapes=[
            pltpu.VMEM((2, capacity, ff), jnp.float32),
            pltpu.VMEM((8, 128), jnp.float32),
            pltpu.SemaphoreType.DMA((n_pieces + 1,)),
        ],
        compiler_params=pltpu.CompilerParams(vmem_limit_bytes=VMEM_BYTES),
        name="gate_up",
    )(rows, gate_mat, up_mat)


def tail_kernel(down_ref, combine_ref, slot_ref, *refs):
    out_ref, sums_ref, sems = refs[-3:]
    pieces = refs[:-4]
    capacity, ff = sums_ref.shape[1:]
    places = piece_places(capacity, ff)
    copies = []
    for half in range(2):
        for k, (r, c) in enumerate(places):
            n = half * len(places) + k
            copy = pltpu.make_async_copy(
                pieces[n], sums_ref.at[half, r : r + PIECE_ROWS, c : c + PIECE_COLS], sems.at[n]
            )
            copy.start()
            copies.append(copy)
    for copy in copies:
        copy.wait()
    gate = sums_ref[0]
    hidden = (gate / (1.0 + jnp.exp(-gate)) * sums_ref[1]).astype(jnp.bfloat16)
    expert_out = jnp.dot(hidden, down_ref[...], preferred_element_type=jnp.float32)
    weighted = (combine_ref[...] * expert_out).astype(jnp.bfloat16)
    slots = out_ref.shape[0]
    slot_ids = lax.broadcasted_iota(jnp.int32, (slots, capacity), 0)
    table = jnp.where(slot_ref[...] == slot_ids, 1.0, 0.0).astype(jnp.bfloat16)
    out_ref[...] = jnp.dot(table, weighted, preferred_element_type=jnp.float32).astype(jnp.bfloat16)


def expert_tail(sums, down_mat, combine, slot, slots):
    ff, width = down_mat.shape
    capacity = combine.shape[0]
    return pl.pallas_call(
        tail_kernel,
        out_shape=jax.ShapeDtypeStruct((slots, width), jnp.bfloat16),
        in_specs=[pl.BlockSpec(memory_space=pltpu.VMEM)] * 3
        + [pl.BlockSpec(memory_space=pltpu.HBM)] * len(sums),
        out_specs=pl.BlockSpec(memory_space=pltpu.VMEM),
        scratch_shapes=[
            pltpu.VMEM((2, capacity, ff), jnp.float32),
            pltpu.SemaphoreType.DMA((len(sums) - 1,)),
        ],
        compiler_params=pltpu.CompilerParams(vmem_limit_bytes=TAIL_VMEM_BYTES),
        name="expert_tail",
    )(down_mat, combine[:, None], slot[None, :], *sums)


def shards(
    picked_rows,
    w_gate,
    w_up,
    w_down,
    combine_gate,
    pick_owner,
    pick_row,
    residual_in,
    norm_gain,
    projection,
):
    my_rows = picked_rows[0]
    capacity = my_rows.shape[0]
    n_groups = pick_owner.shape[0]
    slot_most = max(3 * capacity // n_groups, 2)
    tok_group, width = residual_in.shape
    my_index = lax.axis_index("expert")

    full_projection = lax.all_gather(projection, "expert", axis=0, tiled=True)

    parts = gate_up(my_rows, w_gate[0], w_up[0])

    my_owner = lax.dynamic_index_in_dim(pick_owner, my_index, 0, keepdims=False)
    pick_ids = jnp.arange(capacity, dtype=jnp.int32)
    same_earlier = (my_owner[:, None] == my_owner[None, :]) & (pick_ids[:, None] < pick_ids[None, :])
    my_position = jnp.sum(same_earlier.astype(jnp.int32), axis=0)
    my_slot = my_owner * slot_most + my_position

    mine = pick_owner == my_index
    before = (pick_ids[:, None] < pick_ids[None, :]).astype(jnp.bfloat16)
    position = jnp.dot(
        mine.astype(jnp.bfloat16), before, preferred_element_type=jnp.float32
    ).astype(jnp.int32)
    slot_range = jnp.arange(slot_most, dtype=jnp.int32)
    matches = mine[:, None, :] & (position[:, None, :] == slot_range[None, :, None])
    row_of = jnp.sum(jnp.where(matches, pick_row[:, None, :] + 1, 0), axis=2) - 1
    token_ids = jnp.arange(tok_group, dtype=jnp.int32)
    recv_table = (row_of.reshape(-1)[None, :] == token_ids[:, None]).astype(jnp.bfloat16)

    sums = lax.psum(tuple(parts), "tensor")
    outgoing = expert_tail(sums, w_down[0], combine_gate[0], my_slot, n_groups * slot_most)
    outgoing = outgoing.reshape(n_groups, slot_most, width)
    received = lax.all_to_all(outgoing, "expert", split_axis=0, concat_axis=0, tiled=True)
    moe = jnp.dot(
        recv_table,
        received.reshape(n_groups * slot_most, width),
        preferred_element_type=jnp.float32,
    )
    mixed = residual_in.astype(jnp.float32) + moe
    gained = (mixed * norm_gain[None, :]).astype(jnp.bfloat16)
    full_gained = lax.all_gather(gained, "tensor", axis=1, tiled=True)
    square_total = lax.psum(jnp.sum(mixed * mixed, axis=1), "tensor")
    inverse_rms = lax.rsqrt(square_total / D + 1e-05)
    projected = jnp.dot(full_gained, full_projection, preferred_element_type=jnp.float32)
    return (projected * inverse_rms[:, None]).astype(jnp.bfloat16)


def solution(mesh):
    return jax.shard_map(
        shards,
        mesh=mesh,
        in_specs=(
            P("expert", None, "tensor"),
            P("expert", "tensor", None),
            P("expert", "tensor", None),
            P("expert", None, "tensor"),
            P("expert", None),
            P(),
            P(),
            P("expert", "tensor"),
            P("tensor"),
            P("expert", "tensor"),
        ),
        out_specs=P("expert", "tensor"),
        check_vma=False,
    )
```

```python
import functools

import jax
import jax.numpy as jnp
from jax import lax
from jax.experimental import pallas as pl
from jax.experimental.pallas import tpu as pltpu
from jax.sharding import PartitionSpec as P

D = 6144
PIECE_ROWS = 16
PIECE_COLS = 768
VMEM_BYTES = 48 * 1024 * 1024
TAIL_VMEM_BYTES = 63 * 1024 * 1024
RING_ROWS = 384
EXTRA_ROWS = 16


def piece_places(capacity, ff):
    return [(r, c) for r in range(0, capacity, PIECE_ROWS) for c in range(0, ff, PIECE_COLS)]


def gate_up_kernel(rows_ref, gate_ref, up_ref, *refs):
    spare_ref, parts_ref, spare_part_ref, sems = refs[-4:]
    out_refs = refs[:-4]
    capacity, ff = rows_ref.shape[0], gate_ref.shape[1]
    places = piece_places(capacity, ff)
    spare_part_ref[...] = jnp.zeros_like(spare_part_ref)
    copies = [pltpu.make_async_copy(spare_part_ref, spare_ref, sems.at[len(out_refs)])]
    copies[0].start()
    rows = rows_ref[...]
    for half, weights in enumerate((gate_ref, up_ref)):
        parts_ref[half] = jnp.dot(rows, weights[...], preferred_element_type=jnp.float32)
        for k, (r, c) in enumerate(places):
            n = half * len(places) + k
            copy = pltpu.make_async_copy(
                parts_ref.at[half, r : r + PIECE_ROWS, c : c + PIECE_COLS], out_refs[n], sems.at[n]
            )
            copy.start()
            copies.append(copy)
    for copy in copies:
        copy.wait()


def gate_up(rows, gate_mat, up_mat):
    capacity, ff = rows.shape[0], gate_mat.shape[1]
    n_pieces = 2 * len(piece_places(capacity, ff))
    return pl.pallas_call(
        gate_up_kernel,
        out_shape=[pltpu.HBM((PIECE_ROWS, PIECE_COLS), jnp.float32)] * n_pieces
        + [pltpu.HBM((8, 128), jnp.float32)],
        in_specs=[pl.BlockSpec(memory_space=pltpu.VMEM)] * 3,
        out_specs=[pl.BlockSpec(memory_space=pltpu.HBM)] * (n_pieces + 1),
        scratch_shapes=[
            pltpu.VMEM((2, capacity, ff), jnp.float32),
            pltpu.VMEM((8, 128), jnp.float32),
            pltpu.SemaphoreType.DMA((n_pieces + 1,)),
        ],
        compiler_params=pltpu.CompilerParams(vmem_limit_bytes=VMEM_BYTES),
        name="gate_up",
    )(rows, gate_mat, up_mat)


def tail_kernel(down_ref, combine_ref, slot_ref, *refs):
    out_ref, sums_ref, sems = refs[-3:]
    pieces = refs[:-4]
    capacity, ff = sums_ref.shape[1:]
    places = piece_places(capacity, ff)
    copies = []
    for half in range(2):
        for k, (r, c) in enumerate(places):
            n = half * len(places) + k
            copy = pltpu.make_async_copy(
                pieces[n], sums_ref.at[half, r : r + PIECE_ROWS, c : c + PIECE_COLS], sems.at[n]
            )
            copy.start()
            copies.append(copy)
    for copy in copies:
        copy.wait()
    gate = sums_ref[0]
    hidden = (gate / (1.0 + jnp.exp(-gate)) * sums_ref[1]).astype(jnp.bfloat16)
    expert_out = jnp.dot(hidden, down_ref[...], preferred_element_type=jnp.float32)
    combine = jnp.broadcast_to(combine_ref[...], (128, capacity)).T[:, 0:1]
    weighted = (combine * expert_out).astype(jnp.bfloat16)
    slots = out_ref.shape[0]
    slot_ids = lax.broadcasted_iota(jnp.int32, (slots, capacity), 0)
    table = jnp.where(slot_ref[...] == slot_ids, 1.0, 0.0).astype(jnp.bfloat16)
    out_ref[...] = jnp.dot(table, weighted, preferred_element_type=jnp.float32).astype(jnp.bfloat16)


def expert_tail(sums, down_mat, combine, slot, slots):
    ff, width = down_mat.shape
    capacity = combine.shape[0]
    return pl.pallas_call(
        tail_kernel,
        out_shape=jax.ShapeDtypeStruct((slots, width), jnp.bfloat16),
        in_specs=[pl.BlockSpec(memory_space=pltpu.VMEM)] * 3
        + [pl.BlockSpec(memory_space=pltpu.HBM)] * len(sums),
        out_specs=pl.BlockSpec(memory_space=pltpu.VMEM),
        scratch_shapes=[
            pltpu.VMEM((2, capacity, ff), jnp.float32),
            pltpu.SemaphoreType.DMA((len(sums) - 1,)),
        ],
        compiler_params=pltpu.CompilerParams(vmem_limit_bytes=TAIL_VMEM_BYTES),
        name="expert_tail",
    )(down_mat, combine[None, :], slot[None, :], *sums)


def mix_kernel(residual_ref, received_ref, row_ref, gain_ref, ring_ref, gather_ref):
    tokens, width = residual_ref.shape
    slots = received_ref.shape[0]
    token_ids = lax.broadcasted_iota(jnp.int32, (tokens, slots), 0)
    table = jnp.where(row_ref[...] == token_ids, 1.0, 0.0).astype(jnp.bfloat16)
    moe = jnp.dot(table, received_ref[...], preferred_element_type=jnp.float32)
    mixed = residual_ref[...].astype(jnp.float32) + moe
    gained = (mixed * gain_ref[...]).astype(jnp.bfloat16)
    ring_rows = ring_ref.shape[0]
    rest = tokens - ring_rows
    ring_ref[...] = gained[:ring_rows]
    gather_ref[:rest] = gained[ring_rows:]
    squares = jnp.sum(mixed * mixed, axis=1, keepdims=True)
    flat = jnp.broadcast_to(squares, (tokens, 128)).T[0:1]
    high = flat.astype(jnp.bfloat16).astype(jnp.float32)
    low = flat - high
    lines = [part[:, i : i + width] for part in (high, low) for i in range(0, tokens, width)]
    lines.append(jnp.zeros((EXTRA_ROWS - len(lines), width), jnp.float32))
    gather_ref[rest:] = jnp.concatenate(lines, axis=0).astype(jnp.bfloat16)


def mix(residual, received, row_of, gain, ring_rows):
    tokens, width = residual.shape
    return pl.pallas_call(
        mix_kernel,
        out_shape=[
            jax.ShapeDtypeStruct((ring_rows, width), jnp.bfloat16),
            jax.ShapeDtypeStruct((tokens - ring_rows + EXTRA_ROWS, width), jnp.bfloat16),
        ],
        in_specs=[pl.BlockSpec(memory_space=pltpu.VMEM)] * 4,
        out_specs=[pl.BlockSpec(memory_space=pltpu.VMEM)] * 2,
        compiler_params=pltpu.CompilerParams(vmem_limit_bytes=VMEM_BYTES),
        name="mix",
    )(residual, received, row_of[None, :], gain[None, :])


def final_kernel(gathered_ref, proj_ref, ring_ref, out_ref, acc_ref, squares_ref):
    step = pl.program_id(0)

    @pl.when(step == 0)
    def _():
        acc_ref[...] = jnp.zeros_like(acc_ref)
        squares_ref[...] = jnp.zeros_like(squares_ref)

    per_step, rows, width = gathered_ref.shape
    rest = rows - EXTRA_ROWS
    total = acc_ref[...]
    for z in range(per_step):
        total += jnp.dot(
            gathered_ref[z, :rest],
            proj_ref[z * width : (z + 1) * width],
            preferred_element_type=jnp.float32,
        )
        squares_ref[...] += gathered_ref[z, rest:].astype(jnp.float32)
    acc_ref[...] = total

    @pl.when(step == pl.num_programs(0) - 1)
    def _():
        tokens = out_ref.shape[0]
        ring_rows = tokens - rest
        lines = tokens // width
        columns = []
        for i in range(lines):
            line = squares_ref[i : i + 1] + squares_ref[lines + i : lines + i + 1]
            columns.append(jnp.broadcast_to(line, (128, width)).T[:, 0:1])
        squares = jnp.concatenate(columns, axis=0)
        inverse = lax.rsqrt(squares / D + 1e-05)
        out_ref[:ring_rows] = (ring_ref[...] * inverse[:ring_rows]).astype(jnp.bfloat16)
        out_ref[ring_rows:] = (acc_ref[...] * inverse[ring_rows:]).astype(jnp.bfloat16)


def final(gathered, full_projection, ring_acc, tokens):
    n, rows, width = gathered.shape
    columns = full_projection.shape[1]
    rest = rows - EXTRA_ROWS
    per_step = 4
    return pl.pallas_call(
        final_kernel,
        grid=(n // per_step,),
        out_shape=jax.ShapeDtypeStruct((tokens, columns), jnp.bfloat16),
        in_specs=[
            pl.BlockSpec((per_step, rows, width), lambda i: (i, 0, 0)),
            pl.BlockSpec((per_step * width, columns), lambda i: (i, 0)),
            pl.BlockSpec((tokens - rest, columns), lambda i: (0, 0)),
        ],
        out_specs=pl.BlockSpec((tokens, columns), lambda i: (0, 0)),
        scratch_shapes=[
            pltpu.VMEM((rest, columns), jnp.float32),
            pltpu.VMEM((EXTRA_ROWS, width), jnp.float32),
        ],
        compiler_params=pltpu.CompilerParams(vmem_limit_bytes=TAIL_VMEM_BYTES),
        name="final",
    )(gathered, full_projection, ring_acc)


def ring_projection(rows, full_projection, axis, n):
    me = lax.axis_index(axis)
    width = rows.shape[1]
    onward = [(i, (i + 1) % n) for i in range(n)]
    back = [(i, (i - 1) % n) for i in range(n)]

    def product(block, source):
        part = lax.dynamic_slice_in_dim(full_projection, lax.rem(source, n) * width, width, 0)
        return jnp.dot(block, part, preferred_element_type=jnp.float32)

    total = product(rows, me)
    ahead = behind = rows
    for k in range(1, n // 2 + 1):
        ahead = lax.ppermute(ahead, axis, onward)
        if k < n - k:
            behind = lax.ppermute(behind, axis, back)
        total = total + product(ahead, me + (n - k))
        if k < n - k:
            total = total + product(behind, me + k)
    return total


def shards(
    picked_rows,
    w_gate,
    w_up,
    w_down,
    combine_gate,
    pick_owner,
    pick_row,
    residual_in,
    norm_gain,
    projection,
    n_tensor,
):
    my_rows = picked_rows[0]
    capacity = my_rows.shape[0]
    n_groups = pick_owner.shape[0]
    slot_most = max(3 * capacity // n_groups, 2)
    tok_group, width = residual_in.shape
    my_index = lax.axis_index("expert")

    parts = gate_up(my_rows, w_gate[0], w_up[0])
    spare, projection = lax.optimization_barrier((parts[-1], projection))
    full_projection = lax.all_gather(projection, "expert", axis=0, tiled=True)

    my_owner = lax.dynamic_index_in_dim(pick_owner, my_index, 0, keepdims=False)
    pick_ids = jnp.arange(capacity, dtype=jnp.int32)
    same_earlier = (my_owner[:, None] == my_owner[None, :]) & (pick_ids[:, None] < pick_ids[None, :])
    my_position = jnp.sum(same_earlier.astype(jnp.int32), axis=0)
    my_slot = my_owner * slot_most + my_position

    mine = pick_owner == my_index
    before = (pick_ids[:, None] < pick_ids[None, :]).astype(jnp.bfloat16)
    position = jnp.dot(
        mine.astype(jnp.bfloat16), before, preferred_element_type=jnp.float32
    ).astype(jnp.int32)
    slot_range = jnp.arange(slot_most, dtype=jnp.int32)
    matches = mine[:, None, :] & (position[:, None, :] == slot_range[None, :, None])
    row_of = jnp.sum(jnp.where(matches, pick_row[:, None, :] + 1, 0), axis=2) - 1

    sums = lax.psum((*parts[:-1], spare), "tensor")
    outgoing = expert_tail(sums, w_down[0], combine_gate[0], my_slot, n_groups * slot_most)
    outgoing = outgoing.reshape(n_groups, slot_most, width)
    received = lax.all_to_all(outgoing, "expert", split_axis=0, concat_axis=0, tiled=True)
    ring_rows, gather_rows = mix(
        residual_in,
        received.reshape(n_groups * slot_most, width),
        row_of.reshape(-1),
        norm_gain,
        RING_ROWS,
    )
    gathered = lax.all_gather(gather_rows, "tensor")
    ring_acc = ring_projection(ring_rows, full_projection, "tensor", n_tensor)
    return final(gathered, full_projection, ring_acc, tok_group)


def solution(mesh):
    return jax.shard_map(
        functools.partial(shards, n_tensor=mesh.shape["tensor"]),
        mesh=mesh,
        in_specs=(
            P("expert", None, "tensor"),
            P("expert", "tensor", None),
            P("expert", "tensor", None),
            P("expert", None, "tensor"),
            P("expert", None),
            P(),
            P(),
            P("expert", "tensor"),
            P("tensor"),
            P("expert", "tensor"),
        ),
        out_specs=P("expert", "tensor"),
        check_vma=False,
    )
```

```python
import jax
import jax.numpy as jnp
from jax import lax
from jax.experimental import pallas as pl
from jax.experimental.pallas import tpu as pltpu
from jax.sharding import PartitionSpec as P

D = 6144
PART_TYPE = jnp.bfloat16
VMEM_BYTES = 63 * 1024 * 1024
SPARES = 40
CHUNKS = 2
PART_ROWS = 16


def gate_up_kernel(rows_hbm, gate_hbm, up_hbm, *refs):
    spare_ref, rows_ref, mats_ref, parts_ref, in_sems, out_sems, spare_sems = refs[-7:]
    n_parts = len(refs) - 7 - SPARES
    out_refs, spare_hbms = refs[:n_parts], refs[n_parts:-7]
    capacity, ff = rows_hbm.shape[0], gate_hbm.shape[1]
    cols = ff // CHUNKS
    spare_ref[...] = jnp.zeros_like(spare_ref)
    get_rows = pltpu.make_async_copy(rows_hbm, rows_ref, in_sems.at[2 * CHUNKS])
    get_rows.start()
    gets = []
    for half, mat in enumerate((gate_hbm, up_hbm)):
        for c in range(CHUNKS):
            span = slice(c * cols, (c + 1) * cols)
            gets.append(
                pltpu.make_async_copy(
                    mat.at[:, span], mats_ref.at[half, :, span], in_sems.at[half * CHUNKS + c]
                )
            )
            gets[-1].start()
    spare_puts = [
        pltpu.make_async_copy(spare_ref, spare_hbm, spare_sems.at[n]) for n, spare_hbm in enumerate(spare_hbms)
    ]
    for put in spare_puts:
        put.start()
    get_rows.wait()
    puts = []
    for half in range(2):
        for c in range(CHUNKS):
            span = slice(c * cols, (c + 1) * cols)
            gets[half * CHUNKS + c].wait()
            parts_ref[half * capacity : (half + 1) * capacity, span] = jnp.dot(
                rows_ref[...], mats_ref[half, :, span], preferred_element_type=jnp.float32
            ).astype(parts_ref.dtype)
        for n in range(half * n_parts // 2, (half + 1) * n_parts // 2):
            puts.append(
                pltpu.make_async_copy(
                    parts_ref.at[n * PART_ROWS : (n + 1) * PART_ROWS], out_refs[n], out_sems.at[n]
                )
            )
            puts[-1].start()
    for put in spare_puts + puts:
        put.wait()


def gate_up(rows, gate_mat, up_mat):
    capacity, depth = rows.shape
    ff = gate_mat.shape[1]
    n_parts = 2 * capacity // PART_ROWS
    return pl.pallas_call(
        gate_up_kernel,
        out_shape=[pltpu.HBM((PART_ROWS, ff), PART_TYPE)] * n_parts
        + [pltpu.HBM((16, 128), PART_TYPE)] * SPARES,
        in_specs=[pl.BlockSpec(memory_space=pltpu.HBM)] * 3,
        out_specs=[pl.BlockSpec(memory_space=pltpu.HBM)] * (n_parts + SPARES),
        scratch_shapes=[
            pltpu.VMEM((16, 128), PART_TYPE),
            pltpu.VMEM((capacity, depth), rows.dtype),
            pltpu.VMEM((2, depth, ff), gate_mat.dtype),
            pltpu.VMEM((2 * capacity, ff), PART_TYPE),
            pltpu.SemaphoreType.DMA((2 * CHUNKS + 1,)),
            pltpu.SemaphoreType.DMA((n_parts,)),
            pltpu.SemaphoreType.DMA((SPARES,)),
        ],
        compiler_params=pltpu.CompilerParams(vmem_limit_bytes=VMEM_BYTES),
        name="gate_up",
    )(rows, gate_mat, up_mat)


def tail_kernel(down_hbm, combine_ref, slot_ref, *refs):
    out_ref, sums_ref, down_ref, hidden_ref, sems = refs[-5:]
    capacity = hidden_ref.shape[0]
    half = capacity // PART_ROWS
    sum_hbms = refs[: 2 * half]
    gets = []
    for c in range(half):
        for n in (c, half + c):
            gets.append(
                pltpu.make_async_copy(
                    sum_hbms[n], sums_ref.at[n * PART_ROWS : (n + 1) * PART_ROWS], sems.at[n]
                )
            )
            gets[-1].start()
    get_down = pltpu.make_async_copy(down_hbm, down_ref, sems.at[2 * half])
    get_down.start()
    for c in range(half):
        gets[2 * c].wait()
        gets[2 * c + 1].wait()
        start = c * PART_ROWS
        gate = sums_ref[start : start + PART_ROWS].astype(jnp.float32)
        up = sums_ref[capacity + start : capacity + start + PART_ROWS].astype(jnp.float32)
        hidden_ref[start : start + PART_ROWS] = (gate / (1.0 + jnp.exp(-gate)) * up).astype(jnp.bfloat16)
    get_down.wait()
    expert_out = jnp.dot(hidden_ref[...], down_ref[...], preferred_element_type=jnp.float32)
    combine = jnp.broadcast_to(combine_ref[...], (128, capacity)).T[:, 0:1]
    weighted = (combine * expert_out).astype(jnp.bfloat16)
    slots = out_ref.shape[0]
    slot_ids = lax.broadcasted_iota(jnp.int32, (slots, capacity), 0)
    table = jnp.where(slot_ref[...] == slot_ids, 1.0, 0.0).astype(jnp.bfloat16)
    out_ref[...] = jnp.dot(table, weighted, preferred_element_type=jnp.float32).astype(jnp.bfloat16)


def expert_tail(sums, down_mat, combine, slot, slots):
    ff, width = down_mat.shape
    capacity = combine.shape[0]
    return pl.pallas_call(
        tail_kernel,
        out_shape=jax.ShapeDtypeStruct((slots, width), jnp.bfloat16),
        in_specs=[pl.BlockSpec(memory_space=pltpu.HBM)]
        + [pl.BlockSpec(memory_space=pltpu.VMEM)] * 2
        + [pl.BlockSpec(memory_space=pltpu.HBM)] * len(sums),
        out_specs=pl.BlockSpec(memory_space=pltpu.VMEM),
        scratch_shapes=[
            pltpu.VMEM((2 * capacity, ff), PART_TYPE),
            pltpu.VMEM((ff, width), down_mat.dtype),
            pltpu.VMEM((capacity, ff), jnp.bfloat16),
            pltpu.SemaphoreType.DMA((2 * capacity // PART_ROWS + 1,)),
        ],
        compiler_params=pltpu.CompilerParams(vmem_limit_bytes=VMEM_BYTES),
        name="expert_tail",
    )(down_mat, combine[None, :], slot[None, :], *sums)


def mix_kernel(residual_ref, received_ref, row_ref, gain_ref, out_ref, squares_ref):
    tokens, width = residual_ref.shape
    slots = received_ref.shape[0]
    token_ids = lax.broadcasted_iota(jnp.int32, (tokens, slots), 0)
    table = jnp.where(row_ref[...] == token_ids, 1.0, 0.0).astype(jnp.bfloat16)
    moe = jnp.dot(table, received_ref[...], preferred_element_type=jnp.float32)
    mixed = residual_ref[...].astype(jnp.float32) + moe
    out_ref[...] = (mixed * gain_ref[...]).astype(jnp.bfloat16)
    squares = jnp.sum(mixed * mixed, axis=1, keepdims=True)
    squares_ref[...] = jnp.broadcast_to(squares, (tokens, 128)).T[0:1]


def mix(residual, received, row_of, gain):
    tokens, width = residual.shape
    return pl.pallas_call(
        mix_kernel,
        out_shape=[
            jax.ShapeDtypeStruct((tokens, width), jnp.bfloat16),
            jax.ShapeDtypeStruct((1, tokens), jnp.float32),
        ],
        in_specs=[pl.BlockSpec(memory_space=pltpu.VMEM)] * 4,
        out_specs=[pl.BlockSpec(memory_space=pltpu.VMEM)] * 2,
        compiler_params=pltpu.CompilerParams(vmem_limit_bytes=40 * 1024 * 1024),
        name="mix",
    )(residual, received, row_of[None, :], gain[None, :])


def final_kernel(gathered_ref, proj_ref, squares_ref, out_ref, acc_ref):
    step = pl.program_id(0)
    per_step, tokens, width = gathered_ref.shape
    pair = 2 * width
    total = None
    for z in range(0, per_step, 2):
        block = jnp.concatenate([gathered_ref[z], gathered_ref[z + 1]], axis=1)
        part = jnp.dot(
            block, proj_ref[z * width : z * width + pair], preferred_element_type=jnp.float32
        )
        total = part if total is None else total + part

    @pl.when(step == 0)
    def _():
        acc_ref[...] = total

    @pl.when(step > 0)
    def _():
        acc_ref[...] += total

    @pl.when(step == pl.num_programs(0) - 1)
    def _():
        inverse = lax.rsqrt(squares_ref[...] / D + 1e-05)
        column = jnp.broadcast_to(inverse, (128, tokens)).T[:, 0:1]
        out_ref[...] = (acc_ref[...] * column).astype(jnp.bfloat16)


def final(gathered, full_projection, square_total):
    n, tokens, width = gathered.shape
    columns = full_projection.shape[1]
    per_step = 2
    return pl.pallas_call(
        final_kernel,
        grid=(n // per_step,),
        out_shape=jax.ShapeDtypeStruct((tokens, columns), jnp.bfloat16),
        in_specs=[
            pl.BlockSpec((per_step, tokens, width), lambda i: (i, 0, 0)),
            pl.BlockSpec((per_step * width, columns), lambda i: (i, 0)),
            pl.BlockSpec((1, tokens), lambda i: (0, 0)),
        ],
        out_specs=pl.BlockSpec((tokens, columns), lambda i: (0, 0)),
        scratch_shapes=[pltpu.VMEM((tokens, columns), jnp.float32)],
        compiler_params=pltpu.CompilerParams(vmem_limit_bytes=VMEM_BYTES),
        name="final",
    )(gathered, full_projection, square_total)


def shards(
    picked_rows,
    w_gate,
    w_up,
    w_down,
    combine_gate,
    pick_owner,
    pick_row,
    residual_in,
    norm_gain,
    projection,
):
    my_rows = picked_rows[0]
    capacity = my_rows.shape[0]
    n_groups = pick_owner.shape[0]
    slot_most = max(3 * capacity // n_groups, 2)
    width = residual_in.shape[1]
    my_index = lax.axis_index("expert")

    parts = gate_up(my_rows, w_gate[0], w_up[0])
    full_projection = lax.all_gather(projection, "expert", axis=0, tiled=True)

    my_owner = lax.dynamic_index_in_dim(pick_owner, my_index, 0, keepdims=False)
    pick_ids = jnp.arange(capacity, dtype=jnp.int32)
    same_earlier = (my_owner[:, None] == my_owner[None, :]) & (pick_ids[:, None] < pick_ids[None, :])
    my_position = jnp.sum(same_earlier.astype(jnp.int32), axis=0)
    my_slot = my_owner * slot_most + my_position

    mine = pick_owner == my_index
    before = (pick_ids[:, None] < pick_ids[None, :]).astype(jnp.bfloat16)
    position = jnp.dot(
        mine.astype(jnp.bfloat16), before, preferred_element_type=jnp.float32
    ).astype(jnp.int32)
    slot_range = jnp.arange(slot_most, dtype=jnp.int32)
    matches = mine[:, None, :] & (position[:, None, :] == slot_range[None, :, None])
    row_of = jnp.sum(jnp.where(matches, pick_row[:, None, :] + 1, 0), axis=2) - 1

    sums = lax.psum(tuple(parts), "tensor")
    outgoing = expert_tail(sums, w_down[0], combine_gate[0], my_slot, n_groups * slot_most)
    outgoing = outgoing.reshape(n_groups, slot_most, width)
    received = lax.all_to_all(outgoing, "expert", split_axis=0, concat_axis=0, tiled=True)
    gained, squares = mix(
        residual_in, received.reshape(n_groups * slot_most, width), row_of.reshape(-1), norm_gain
    )
    full_gained = lax.all_gather(gained, "tensor")
    square_total = lax.psum(squares, "tensor")
    return final(full_gained, full_projection, square_total)


def solution(mesh):
    return jax.shard_map(
        shards,
        mesh=mesh,
        in_specs=(
            P("expert", None, "tensor"),
            P("expert", "tensor", None),
            P("expert", "tensor", None),
            P("expert", None, "tensor"),
            P("expert", None),
            P(),
            P(),
            P("expert", "tensor"),
            P("tensor"),
            P("expert", "tensor"),
        ),
        out_specs=P("expert", "tensor"),
        check_vma=False,
    )
```

```python
import jax
import jax.numpy as jnp
from jax import lax
from jax.experimental import pallas as pl
from jax.experimental.pallas import tpu as pltpu
from jax.sharding import PartitionSpec as P

D = 6144
PART_TYPE = jnp.bfloat16
VMEM_BYTES = 63 * 1024 * 1024
SPARES = 33
CHUNKS = 1
PART_ROWS = 16


def gate_up_kernel(rows_hbm, gate_hbm, up_hbm, *refs):
    spare_ref, rows_ref, mats_ref, parts_ref, in_sems, out_sems, spare_sems = refs[-7:]
    n_parts = len(refs) - 7 - SPARES
    out_refs, spare_hbms = refs[:n_parts], refs[n_parts:-7]
    capacity, ff = rows_hbm.shape[0], gate_hbm.shape[1]
    cols = ff // CHUNKS
    spare_ref[...] = jnp.zeros_like(spare_ref)
    get_rows = pltpu.make_async_copy(rows_hbm, rows_ref, in_sems.at[2 * CHUNKS])
    get_rows.start()
    gets = []
    for half, mat in enumerate((gate_hbm, up_hbm)):
        for c in range(CHUNKS):
            span = slice(c * cols, (c + 1) * cols)
            gets.append(
                pltpu.make_async_copy(
                    mat.at[:, span], mats_ref.at[half, :, span], in_sems.at[half * CHUNKS + c]
                )
            )
            gets[-1].start()
    spare_puts = [
        pltpu.make_async_copy(spare_ref, spare_hbm, spare_sems.at[n]) for n, spare_hbm in enumerate(spare_hbms)
    ]
    get_rows.wait()
    puts = []
    for half in range(2):
        for c in range(CHUNKS):
            span = slice(c * cols, (c + 1) * cols)
            gets[half * CHUNKS + c].wait()
            parts_ref[half * capacity : (half + 1) * capacity, span] = jnp.dot(
                rows_ref[...], mats_ref[half, :, span], preferred_element_type=jnp.float32
            ).astype(parts_ref.dtype)
        for n in range(half * n_parts // 2, (half + 1) * n_parts // 2):
            puts.append(
                pltpu.make_async_copy(
                    parts_ref.at[n * PART_ROWS : (n + 1) * PART_ROWS], out_refs[n], out_sems.at[n]
                )
            )
            puts[-1].start()
    for put in spare_puts:
        put.start()
    for put in spare_puts + puts:
        put.wait()


def gate_up(rows, gate_mat, up_mat):
    capacity, depth = rows.shape
    ff = gate_mat.shape[1]
    n_parts = 2 * capacity // PART_ROWS
    return pl.pallas_call(
        gate_up_kernel,
        out_shape=[pltpu.HBM((PART_ROWS, ff), PART_TYPE)] * n_parts
        + [pltpu.HBM((16, 128), PART_TYPE)] * SPARES,
        in_specs=[pl.BlockSpec(memory_space=pltpu.HBM)] * 3,
        out_specs=[pl.BlockSpec(memory_space=pltpu.HBM)] * (n_parts + SPARES),
        scratch_shapes=[
            pltpu.VMEM((16, 128), PART_TYPE),
            pltpu.VMEM((capacity, depth), rows.dtype),
            pltpu.VMEM((2, depth, ff), gate_mat.dtype),
            pltpu.VMEM((2 * capacity, ff), PART_TYPE),
            pltpu.SemaphoreType.DMA((2 * CHUNKS + 1,)),
            pltpu.SemaphoreType.DMA((n_parts,)),
            pltpu.SemaphoreType.DMA((SPARES,)),
        ],
        compiler_params=pltpu.CompilerParams(vmem_limit_bytes=VMEM_BYTES),
        name="gate_up",
    )(rows, gate_mat, up_mat)


def tail_kernel(down_hbm, combine_ref, slot_ref, *refs):
    out_ref, sums_ref, down_ref, hidden_ref, sems = refs[-5:]
    capacity = hidden_ref.shape[0]
    half = capacity // PART_ROWS
    sum_hbms = refs[: 2 * half]
    gets = []
    for c in range(half):
        for n in (c, half + c):
            gets.append(
                pltpu.make_async_copy(
                    sum_hbms[n], sums_ref.at[n * PART_ROWS : (n + 1) * PART_ROWS], sems.at[n]
                )
            )
            gets[-1].start()
    get_down = pltpu.make_async_copy(down_hbm, down_ref, sems.at[2 * half])
    get_down.start()
    for c in range(half):
        gets[2 * c].wait()
        gets[2 * c + 1].wait()
        start = c * PART_ROWS
        gate = sums_ref[start : start + PART_ROWS].astype(jnp.float32)
        up = sums_ref[capacity + start : capacity + start + PART_ROWS].astype(jnp.float32)
        hidden_ref[start : start + PART_ROWS] = (gate / (1.0 + jnp.exp(-gate)) * up).astype(jnp.bfloat16)
    get_down.wait()
    expert_out = jnp.dot(hidden_ref[...], down_ref[...], preferred_element_type=jnp.float32)
    combine = jnp.broadcast_to(combine_ref[...], (128, capacity)).T[:, 0:1]
    weighted = (combine * expert_out).astype(jnp.bfloat16)
    slots = out_ref.shape[0]
    slot_ids = lax.broadcasted_iota(jnp.int32, (slots, capacity), 0)
    table = jnp.where(slot_ref[...] == slot_ids, 1.0, 0.0).astype(jnp.bfloat16)
    out_ref[...] = jnp.dot(table, weighted, preferred_element_type=jnp.float32).astype(jnp.bfloat16)


def expert_tail(sums, down_mat, combine, slot, slots):
    ff, width = down_mat.shape
    capacity = combine.shape[0]
    return pl.pallas_call(
        tail_kernel,
        out_shape=jax.ShapeDtypeStruct((slots, width), jnp.bfloat16),
        in_specs=[pl.BlockSpec(memory_space=pltpu.HBM)]
        + [pl.BlockSpec(memory_space=pltpu.VMEM)] * 2
        + [pl.BlockSpec(memory_space=pltpu.HBM)] * len(sums),
        out_specs=pl.BlockSpec(memory_space=pltpu.VMEM),
        scratch_shapes=[
            pltpu.VMEM((2 * capacity, ff), PART_TYPE),
            pltpu.VMEM((ff, width), down_mat.dtype),
            pltpu.VMEM((capacity, ff), jnp.bfloat16),
            pltpu.SemaphoreType.DMA((2 * capacity // PART_ROWS + 1,)),
        ],
        compiler_params=pltpu.CompilerParams(vmem_limit_bytes=VMEM_BYTES),
        name="expert_tail",
    )(down_mat, combine[None, :], slot[None, :], *sums)


def mix_kernel(residual_ref, received_ref, row_ref, gain_ref, out_ref, squares_ref):
    tokens, width = residual_ref.shape
    slots = received_ref.shape[0]
    token_ids = lax.broadcasted_iota(jnp.int32, (tokens, slots), 0)
    table = jnp.where(row_ref[...] == token_ids, 1.0, 0.0).astype(jnp.bfloat16)
    moe = jnp.dot(table, received_ref[...], preferred_element_type=jnp.float32)
    mixed = residual_ref[...].astype(jnp.float32) + moe
    out_ref[...] = (mixed * gain_ref[...]).astype(jnp.bfloat16)
    squares = jnp.sum(mixed * mixed, axis=1, keepdims=True)
    squares_ref[...] = jnp.broadcast_to(squares, (tokens, 128)).T[0:1]


def mix(residual, received, row_of, gain):
    tokens, width = residual.shape
    return pl.pallas_call(
        mix_kernel,
        out_shape=[
            jax.ShapeDtypeStruct((tokens, width), jnp.bfloat16),
            jax.ShapeDtypeStruct((1, tokens), jnp.float32),
        ],
        in_specs=[pl.BlockSpec(memory_space=pltpu.VMEM)] * 4,
        out_specs=[pl.BlockSpec(memory_space=pltpu.VMEM)] * 2,
        compiler_params=pltpu.CompilerParams(vmem_limit_bytes=40 * 1024 * 1024),
        name="mix",
    )(residual, received, row_of[None, :], gain[None, :])


def final_kernel(gathered_ref, proj_ref, squares_ref, out_ref, acc_ref):
    step = pl.program_id(0)
    per_step, tokens, width = gathered_ref.shape
    block = jnp.concatenate([gathered_ref[z] for z in range(per_step)], axis=1)
    total = jnp.dot(block, proj_ref[...], preferred_element_type=jnp.float32)

    @pl.when(step == 0)
    def _():
        acc_ref[...] = total

    @pl.when(step > 0)
    def _():
        acc_ref[...] += total

    @pl.when(step == pl.num_programs(0) - 1)
    def _():
        inverse = lax.rsqrt(squares_ref[...] / D + 1e-05)
        column = jnp.broadcast_to(inverse, (128, tokens)).T[:, 0:1]
        out_ref[...] = (acc_ref[...] * column).astype(jnp.bfloat16)


def final(gathered, full_projection, square_total):
    n, tokens, width = gathered.shape
    columns = full_projection.shape[1]
    per_step = 8
    return pl.pallas_call(
        final_kernel,
        grid=(n // per_step,),
        out_shape=jax.ShapeDtypeStruct((tokens, columns), jnp.bfloat16),
        in_specs=[
            pl.BlockSpec((per_step, tokens, width), lambda i: (i, 0, 0)),
            pl.BlockSpec((per_step * width, columns), lambda i: (i, 0)),
            pl.BlockSpec((1, tokens), lambda i: (0, 0)),
        ],
        out_specs=pl.BlockSpec((tokens, columns), lambda i: (0, 0)),
        scratch_shapes=[pltpu.VMEM((tokens, columns), jnp.float32)],
        compiler_params=pltpu.CompilerParams(vmem_limit_bytes=VMEM_BYTES),
        name="final",
    )(gathered, full_projection, square_total)


def shards(
    picked_rows,
    w_gate,
    w_up,
    w_down,
    combine_gate,
    pick_owner,
    pick_row,
    residual_in,
    norm_gain,
    projection,
):
    my_rows = picked_rows[0]
    capacity = my_rows.shape[0]
    n_groups = pick_owner.shape[0]
    slot_most = max(3 * capacity // n_groups, 2)
    width = residual_in.shape[1]
    my_index = lax.axis_index("expert")

    parts = gate_up(my_rows, w_gate[0], w_up[0])

    my_owner = lax.dynamic_index_in_dim(pick_owner, my_index, 0, keepdims=False)
    pick_ids = jnp.arange(capacity, dtype=jnp.int32)
    same_earlier = (my_owner[:, None] == my_owner[None, :]) & (pick_ids[:, None] < pick_ids[None, :])
    my_position = jnp.sum(same_earlier.astype(jnp.int32), axis=0)
    my_slot = my_owner * slot_most + my_position

    mine = pick_owner == my_index
    before = (pick_ids[:, None] < pick_ids[None, :]).astype(jnp.bfloat16)
    position = jnp.dot(
        mine.astype(jnp.bfloat16), before, preferred_element_type=jnp.float32
    ).astype(jnp.int32)
    slot_range = jnp.arange(slot_most, dtype=jnp.int32)
    matches = mine[:, None, :] & (position[:, None, :] == slot_range[None, :, None])
    row_of = jnp.sum(jnp.where(matches, pick_row[:, None, :] + 1, 0), axis=2) - 1

    sums = lax.psum(tuple(parts), "tensor")
    outgoing = expert_tail(sums, w_down[0], combine_gate[0], my_slot, n_groups * slot_most)
    outgoing = outgoing.reshape(n_groups, slot_most, width)
    received = lax.all_to_all(outgoing, "expert", split_axis=0, concat_axis=0, tiled=True)
    gained, squares = mix(
        residual_in, received.reshape(n_groups * slot_most, width), row_of.reshape(-1), norm_gain
    )
    full_gained = lax.all_gather(gained, "tensor")
    square_total = lax.psum(squares, "tensor")
    square_total, projection = lax.optimization_barrier((square_total, projection))
    copies = jnp.broadcast_to(projection[None], (n_groups, *projection.shape))
    full_projection = lax.all_to_all(copies, "expert", split_axis=0, concat_axis=0, tiled=True)
    full_projection = full_projection.reshape(n_groups * projection.shape[0], width)
    return final(full_gained, full_projection, square_total)


def solution(mesh):
    return jax.shard_map(
        shards,
        mesh=mesh,
        in_specs=(
            P("expert", None, "tensor"),
            P("expert", "tensor", None),
            P("expert", "tensor", None),
            P("expert", None, "tensor"),
            P("expert", None),
            P(),
            P(),
            P("expert", "tensor"),
            P("tensor"),
            P("expert", "tensor"),
        ),
        out_specs=P("expert", "tensor"),
        check_vma=False,
    )
```

```python
import jax
import jax.numpy as jnp
from jax import lax
from jax.experimental import pallas as pl
from jax.experimental.pallas import tpu as pltpu
from jax.sharding import PartitionSpec as P

D = 6144
PART_TYPE = jnp.bfloat16
VMEM_BYTES = 63 * 1024 * 1024
SPARES = 33
CHUNKS = 1
PART_ROWS = 16


def gate_up_kernel(rows_hbm, gate_hbm, up_hbm, *refs):
    spare_ref, rows_ref, mats_ref, parts_ref, in_sems, out_sems, spare_sems = refs[-7:]
    n_parts = len(refs) - 7 - SPARES
    out_refs, spare_hbms = refs[:n_parts], refs[n_parts:-7]
    capacity, ff = rows_hbm.shape[0], gate_hbm.shape[1]
    cols = ff // CHUNKS
    spare_ref[...] = jnp.zeros_like(spare_ref)
    get_rows = pltpu.make_async_copy(rows_hbm, rows_ref, in_sems.at[2 * CHUNKS])
    get_rows.start()
    gets = []
    for half, mat in enumerate((gate_hbm, up_hbm)):
        for c in range(CHUNKS):
            span = slice(c * cols, (c + 1) * cols)
            gets.append(
                pltpu.make_async_copy(
                    mat.at[:, span], mats_ref.at[half, :, span], in_sems.at[half * CHUNKS + c]
                )
            )
            gets[-1].start()
    spare_puts = [
        pltpu.make_async_copy(spare_ref, spare_hbm, spare_sems.at[n]) for n, spare_hbm in enumerate(spare_hbms)
    ]
    get_rows.wait()
    puts = []
    for half in range(2):
        for c in range(CHUNKS):
            span = slice(c * cols, (c + 1) * cols)
            gets[half * CHUNKS + c].wait()
            parts_ref[half * capacity : (half + 1) * capacity, span] = jnp.dot(
                rows_ref[...], mats_ref[half, :, span], preferred_element_type=jnp.float32
            ).astype(parts_ref.dtype)
        for n in range(half * n_parts // 2, (half + 1) * n_parts // 2):
            puts.append(
                pltpu.make_async_copy(
                    parts_ref.at[n * PART_ROWS : (n + 1) * PART_ROWS], out_refs[n], out_sems.at[n]
                )
            )
            puts[-1].start()
    for put in spare_puts:
        put.start()
    for put in spare_puts + puts:
        put.wait()


def gate_up(rows, gate_mat, up_mat):
    capacity, depth = rows.shape
    ff = gate_mat.shape[1]
    n_parts = 2 * capacity // PART_ROWS
    return pl.pallas_call(
        gate_up_kernel,
        out_shape=[pltpu.HBM((PART_ROWS, ff), PART_TYPE)] * n_parts
        + [pltpu.HBM((16, 128), PART_TYPE)] * SPARES,
        in_specs=[pl.BlockSpec(memory_space=pltpu.HBM)] * 3,
        out_specs=[pl.BlockSpec(memory_space=pltpu.HBM)] * (n_parts + SPARES),
        scratch_shapes=[
            pltpu.VMEM((16, 128), PART_TYPE),
            pltpu.VMEM((capacity, depth), rows.dtype),
            pltpu.VMEM((2, depth, ff), gate_mat.dtype),
            pltpu.VMEM((2 * capacity, ff), PART_TYPE),
            pltpu.SemaphoreType.DMA((2 * CHUNKS + 1,)),
            pltpu.SemaphoreType.DMA((n_parts,)),
            pltpu.SemaphoreType.DMA((SPARES,)),
        ],
        compiler_params=pltpu.CompilerParams(vmem_limit_bytes=VMEM_BYTES),
        name="gate_up",
    )(rows, gate_mat, up_mat)


def tail_kernel(down_hbm, combine_ref, owner_ref, *refs):
    out_ref, sums_ref, down_ref, hidden_ref, sems = refs[-5:]
    capacity = hidden_ref.shape[0]
    half = capacity // PART_ROWS
    sum_hbms = refs[: 2 * half]
    gets = []
    for c in range(half):
        for n in (c, half + c):
            gets.append(
                pltpu.make_async_copy(
                    sum_hbms[n], sums_ref.at[n * PART_ROWS : (n + 1) * PART_ROWS], sems.at[n]
                )
            )
            gets[-1].start()
    slots = out_ref.shape[0]
    owners = owner_ref[pl.ds(lax.axis_index("expert"), 1)].astype(jnp.float32)
    owner_column = jnp.broadcast_to(owners, (128, capacity)).T[:, 0:1]
    pick_row = lax.broadcasted_iota(jnp.int32, (capacity, capacity), 0)
    pick_column = lax.broadcasted_iota(jnp.int32, (capacity, capacity), 1)
    earlier = (owner_column == owners) & (pick_row < pick_column)
    position = jnp.sum(jnp.where(earlier, 1.0, 0.0), axis=0, keepdims=True)
    slot = (owners * (slots // owner_ref.shape[0]) + position).astype(jnp.int32)
    get_down = pltpu.make_async_copy(down_hbm, down_ref, sems.at[2 * half])
    get_down.start()
    for c in range(half):
        gets[2 * c].wait()
        gets[2 * c + 1].wait()
        start = c * PART_ROWS
        gate = sums_ref[start : start + PART_ROWS].astype(jnp.float32)
        up = sums_ref[capacity + start : capacity + start + PART_ROWS].astype(jnp.float32)
        hidden_ref[start : start + PART_ROWS] = (gate / (1.0 + jnp.exp(-gate)) * up).astype(jnp.bfloat16)
    get_down.wait()
    expert_out = jnp.dot(hidden_ref[...], down_ref[...], preferred_element_type=jnp.float32)
    combine = jnp.broadcast_to(combine_ref[...], (128, capacity)).T[:, 0:1]
    weighted = (combine * expert_out).astype(jnp.bfloat16)
    slot_ids = lax.broadcasted_iota(jnp.int32, (slots, capacity), 0)
    table = jnp.where(slot == slot_ids, 1.0, 0.0).astype(jnp.bfloat16)
    out_ref[...] = jnp.dot(table, weighted, preferred_element_type=jnp.float32).astype(jnp.bfloat16)


def expert_tail(sums, down_mat, combine, pick_owner, slots):
    ff, width = down_mat.shape
    capacity = combine.shape[0]
    return pl.pallas_call(
        tail_kernel,
        out_shape=jax.ShapeDtypeStruct((slots, width), jnp.bfloat16),
        in_specs=[pl.BlockSpec(memory_space=pltpu.HBM)]
        + [pl.BlockSpec(memory_space=pltpu.VMEM)] * 2
        + [pl.BlockSpec(memory_space=pltpu.HBM)] * len(sums),
        out_specs=pl.BlockSpec(memory_space=pltpu.VMEM),
        scratch_shapes=[
            pltpu.VMEM((2 * capacity, ff), PART_TYPE),
            pltpu.VMEM((ff, width), down_mat.dtype),
            pltpu.VMEM((capacity, ff), jnp.bfloat16),
            pltpu.SemaphoreType.DMA((2 * capacity // PART_ROWS + 1,)),
        ],
        compiler_params=pltpu.CompilerParams(vmem_limit_bytes=VMEM_BYTES),
        name="expert_tail",
    )(down_mat, combine[None, :], pick_owner, *sums)


def mix_kernel(residual_ref, received_ref, row_ref, gain_ref, out_ref, squares_ref):
    tokens, width = residual_ref.shape
    slots = received_ref.shape[0]
    token_ids = lax.broadcasted_iota(jnp.int32, (tokens, slots), 0)
    table = jnp.where(row_ref[...] == token_ids, 1.0, 0.0).astype(jnp.bfloat16)
    moe = jnp.dot(table, received_ref[...], preferred_element_type=jnp.float32)
    mixed = residual_ref[...].astype(jnp.float32) + moe
    out_ref[...] = (mixed * gain_ref[...]).astype(jnp.bfloat16)
    squares = jnp.sum(mixed * mixed, axis=1, keepdims=True)
    squares_ref[...] = jnp.broadcast_to(squares, (tokens, 128)).T[0:1]


def mix(residual, received, row_of, gain):
    tokens, width = residual.shape
    return pl.pallas_call(
        mix_kernel,
        out_shape=[
            jax.ShapeDtypeStruct((tokens, width), jnp.bfloat16),
            jax.ShapeDtypeStruct((1, tokens), jnp.float32),
        ],
        in_specs=[pl.BlockSpec(memory_space=pltpu.VMEM)] * 4,
        out_specs=[pl.BlockSpec(memory_space=pltpu.VMEM)] * 2,
        compiler_params=pltpu.CompilerParams(vmem_limit_bytes=40 * 1024 * 1024),
        name="mix",
    )(residual, received, row_of[None, :], gain[None, :])


def final_kernel(gathered_ref, proj_ref, squares_ref, out_ref, acc_ref):
    step = pl.program_id(0)
    per_step, tokens, width = gathered_ref.shape
    block = jnp.concatenate([gathered_ref[z] for z in range(per_step)], axis=1)
    total = jnp.dot(block, proj_ref[...], preferred_element_type=jnp.float32)

    @pl.when(step == 0)
    def _():
        acc_ref[...] = total

    @pl.when(step > 0)
    def _():
        acc_ref[...] += total

    @pl.when(step == pl.num_programs(0) - 1)
    def _():
        inverse = lax.rsqrt(squares_ref[...] / D + 1e-05)
        column = jnp.broadcast_to(inverse, (128, tokens)).T[:, 0:1]
        out_ref[...] = (acc_ref[...] * column).astype(jnp.bfloat16)


def final(gathered, full_projection, square_total):
    n, tokens, width = gathered.shape
    columns = full_projection.shape[1]
    per_step = 8
    return pl.pallas_call(
        final_kernel,
        grid=(n // per_step,),
        out_shape=jax.ShapeDtypeStruct((tokens, columns), jnp.bfloat16),
        in_specs=[
            pl.BlockSpec((per_step, tokens, width), lambda i: (i, 0, 0)),
            pl.BlockSpec((per_step * width, columns), lambda i: (i, 0)),
            pl.BlockSpec((1, tokens), lambda i: (0, 0)),
        ],
        out_specs=pl.BlockSpec((tokens, columns), lambda i: (0, 0)),
        scratch_shapes=[pltpu.VMEM((tokens, columns), jnp.float32)],
        compiler_params=pltpu.CompilerParams(vmem_limit_bytes=VMEM_BYTES),
        name="final",
    )(gathered, full_projection, square_total)


def shards(
    picked_rows,
    w_gate,
    w_up,
    w_down,
    combine_gate,
    pick_owner,
    pick_row,
    residual_in,
    norm_gain,
    projection,
):
    my_rows = picked_rows[0]
    capacity = my_rows.shape[0]
    n_groups = pick_owner.shape[0]
    slot_most = max(3 * capacity // n_groups, 2)
    width = residual_in.shape[1]
    my_index = lax.axis_index("expert")

    parts = gate_up(my_rows, w_gate[0], w_up[0])

    pick_ids = jnp.arange(capacity, dtype=jnp.int32)

    mine = pick_owner == my_index
    before = (pick_ids[:, None] < pick_ids[None, :]).astype(jnp.bfloat16)
    position = jnp.dot(
        mine.astype(jnp.bfloat16), before, preferred_element_type=jnp.float32
    ).astype(jnp.int32)
    slot_range = jnp.arange(slot_most, dtype=jnp.int32)
    matches = mine[:, None, :] & (position[:, None, :] == slot_range[None, :, None])
    row_of = jnp.sum(jnp.where(matches, pick_row[:, None, :] + 1, 0), axis=2) - 1

    sums = lax.psum(tuple(parts), "tensor")
    outgoing = expert_tail(sums, w_down[0], combine_gate[0], pick_owner, n_groups * slot_most)
    outgoing = outgoing.reshape(n_groups, slot_most, width)
    received = lax.all_to_all(outgoing, "expert", split_axis=0, concat_axis=0, tiled=True)
    gained, squares = mix(
        residual_in, received.reshape(n_groups * slot_most, width), row_of.reshape(-1), norm_gain
    )
    full_gained = lax.all_gather(gained, "tensor")
    square_total = lax.psum(squares, "tensor")
    square_total, projection = lax.optimization_barrier((square_total, projection))
    copies = jnp.broadcast_to(projection[None], (n_groups, *projection.shape))
    full_projection = lax.all_to_all(copies, "expert", split_axis=0, concat_axis=0, tiled=True)
    full_projection = full_projection.reshape(n_groups * projection.shape[0], width)
    return final(full_gained, full_projection, square_total)


def solution(mesh):
    return jax.shard_map(
        shards,
        mesh=mesh,
        in_specs=(
            P("expert", None, "tensor"),
            P("expert", "tensor", None),
            P("expert", "tensor", None),
            P("expert", None, "tensor"),
            P("expert", None),
            P(),
            P(),
            P("expert", "tensor"),
            P("tensor"),
            P("expert", "tensor"),
        ),
        out_specs=P("expert", "tensor"),
        check_vma=False,
    )
```

```python
import functools

import jax
import jax.numpy as jnp
from jax import lax
from jax.experimental import pallas as pl
from jax.experimental.pallas import tpu as pltpu
from jax.sharding import PartitionSpec as P

D = 6144
PART_TYPE = jnp.bfloat16
VMEM_BYTES = 63 * 1024 * 1024
SPARES = 33
EXTRA_ROWS = 16
CHUNKS = 1
PART_ROWS = 16


def gate_up_kernel(rows_hbm, gate_hbm, up_hbm, *refs):
    spare_ref, rows_ref, mats_ref, parts_ref, in_sems, out_sems, spare_sems = refs[-7:]
    n_parts = len(refs) - 7 - SPARES
    out_refs, spare_hbms = refs[:n_parts], refs[n_parts:-7]
    capacity, ff = rows_hbm.shape[0], gate_hbm.shape[1]
    cols = ff // CHUNKS
    spare_ref[...] = jnp.zeros_like(spare_ref)
    get_rows = pltpu.make_async_copy(rows_hbm, rows_ref, in_sems.at[2 * CHUNKS])
    get_rows.start()
    gets = []
    for half, mat in enumerate((gate_hbm, up_hbm)):
        for c in range(CHUNKS):
            span = slice(c * cols, (c + 1) * cols)
            gets.append(
                pltpu.make_async_copy(
                    mat.at[:, span], mats_ref.at[half, :, span], in_sems.at[half * CHUNKS + c]
                )
            )
            gets[-1].start()
    spare_puts = [
        pltpu.make_async_copy(spare_ref, spare_hbm, spare_sems.at[n]) for n, spare_hbm in enumerate(spare_hbms)
    ]
    get_rows.wait()
    puts = []
    for half in range(2):
        for c in range(CHUNKS):
            span = slice(c * cols, (c + 1) * cols)
            gets[half * CHUNKS + c].wait()
            parts_ref[half * capacity : (half + 1) * capacity, span] = jnp.dot(
                rows_ref[...], mats_ref[half, :, span], preferred_element_type=jnp.float32
            ).astype(parts_ref.dtype)
        for n in range(half * n_parts // 2, (half + 1) * n_parts // 2):
            puts.append(
                pltpu.make_async_copy(
                    parts_ref.at[n * PART_ROWS : (n + 1) * PART_ROWS], out_refs[n], out_sems.at[n]
                )
            )
            puts[-1].start()
    for put in spare_puts:
        put.start()
    for put in spare_puts + puts:
        put.wait()


def gate_up(rows, gate_mat, up_mat):
    capacity, depth = rows.shape
    ff = gate_mat.shape[1]
    n_parts = 2 * capacity // PART_ROWS
    return pl.pallas_call(
        gate_up_kernel,
        out_shape=[pltpu.HBM((PART_ROWS, ff), PART_TYPE)] * n_parts
        + [pltpu.HBM((16, 128), PART_TYPE)] * SPARES,
        in_specs=[pl.BlockSpec(memory_space=pltpu.HBM)] * 3,
        out_specs=[pl.BlockSpec(memory_space=pltpu.HBM)] * (n_parts + SPARES),
        scratch_shapes=[
            pltpu.VMEM((16, 128), PART_TYPE),
            pltpu.VMEM((capacity, depth), rows.dtype),
            pltpu.VMEM((2, depth, ff), gate_mat.dtype),
            pltpu.VMEM((2 * capacity, ff), PART_TYPE),
            pltpu.SemaphoreType.DMA((2 * CHUNKS + 1,)),
            pltpu.SemaphoreType.DMA((n_parts,)),
            pltpu.SemaphoreType.DMA((SPARES,)),
        ],
        compiler_params=pltpu.CompilerParams(vmem_limit_bytes=VMEM_BYTES),
        name="gate_up",
    )(rows, gate_mat, up_mat)


def tail_kernel(down_hbm, combine_ref, owner_ref, *refs):
    out_ref, sums_ref, down_ref, hidden_ref, sems = refs[-5:]
    capacity = hidden_ref.shape[0]
    half = capacity // PART_ROWS
    sum_hbms = refs[: 2 * half]
    gets = []
    for c in range(half):
        for n in (c, half + c):
            gets.append(
                pltpu.make_async_copy(
                    sum_hbms[n], sums_ref.at[n * PART_ROWS : (n + 1) * PART_ROWS], sems.at[n]
                )
            )
            gets[-1].start()
    slots = out_ref.shape[0]
    owners = owner_ref[pl.ds(lax.axis_index("expert"), 1)].astype(jnp.float32)
    owner_column = jnp.broadcast_to(owners, (128, capacity)).T[:, 0:1]
    pick_row = lax.broadcasted_iota(jnp.int32, (capacity, capacity), 0)
    pick_column = lax.broadcasted_iota(jnp.int32, (capacity, capacity), 1)
    earlier = (owner_column == owners) & (pick_row < pick_column)
    position = jnp.sum(jnp.where(earlier, 1.0, 0.0), axis=0, keepdims=True)
    slot = (owners * (slots // owner_ref.shape[0]) + position).astype(jnp.int32)
    get_down = pltpu.make_async_copy(down_hbm, down_ref, sems.at[2 * half])
    get_down.start()
    for c in range(half):
        gets[2 * c].wait()
        gets[2 * c + 1].wait()
        start = c * PART_ROWS
        gate = sums_ref[start : start + PART_ROWS].astype(jnp.float32)
        up = sums_ref[capacity + start : capacity + start + PART_ROWS].astype(jnp.float32)
        hidden_ref[start : start + PART_ROWS] = (gate / (1.0 + jnp.exp(-gate)) * up).astype(jnp.bfloat16)
    get_down.wait()
    expert_out = jnp.dot(hidden_ref[...], down_ref[...], preferred_element_type=jnp.float32)
    combine = jnp.broadcast_to(combine_ref[...], (128, capacity)).T[:, 0:1]
    weighted = (combine * expert_out).astype(jnp.bfloat16)
    slot_ids = lax.broadcasted_iota(jnp.int32, (slots, capacity), 0)
    table = jnp.where(slot == slot_ids, 1.0, 0.0).astype(jnp.bfloat16)
    out_ref[...] = jnp.dot(table, weighted, preferred_element_type=jnp.float32).astype(jnp.bfloat16)


def expert_tail(sums, down_mat, combine, pick_owner, slots):
    ff, width = down_mat.shape
    capacity = combine.shape[0]
    return pl.pallas_call(
        tail_kernel,
        out_shape=jax.ShapeDtypeStruct((slots, width), jnp.bfloat16),
        in_specs=[pl.BlockSpec(memory_space=pltpu.HBM)]
        + [pl.BlockSpec(memory_space=pltpu.VMEM)] * 2
        + [pl.BlockSpec(memory_space=pltpu.HBM)] * len(sums),
        out_specs=pl.BlockSpec(memory_space=pltpu.VMEM),
        scratch_shapes=[
            pltpu.VMEM((2 * capacity, ff), PART_TYPE),
            pltpu.VMEM((ff, width), down_mat.dtype),
            pltpu.VMEM((capacity, ff), jnp.bfloat16),
            pltpu.SemaphoreType.DMA((2 * capacity // PART_ROWS + 1,)),
        ],
        compiler_params=pltpu.CompilerParams(vmem_limit_bytes=VMEM_BYTES),
        name="expert_tail",
    )(down_mat, combine[None, :], pick_owner, *sums)


def mix_kernel(residual_ref, received_ref, row_ref, gain_ref, first_ref, second_ref):
    tokens, width = residual_ref.shape
    slots = received_ref.shape[0]
    token_ids = lax.broadcasted_iota(jnp.int32, (tokens, slots), 0)
    table = jnp.where(row_ref[...] == token_ids, 1.0, 0.0).astype(jnp.bfloat16)
    moe = jnp.dot(table, received_ref[...], preferred_element_type=jnp.float32)
    mixed = residual_ref[...].astype(jnp.float32) + moe
    gained = (mixed * gain_ref[...]).astype(jnp.bfloat16)
    half = second_ref.shape[0]
    first_ref[:half] = gained[:half]
    second_ref[...] = gained[half:]
    squares = jnp.sum(mixed * mixed, axis=1, keepdims=True)
    flat = jnp.broadcast_to(squares, (tokens, 128)).T[0:1]
    high = flat.astype(jnp.bfloat16).astype(jnp.float32)
    low = flat - high
    lines = [part[:, i : i + width] for part in (high, low) for i in range(0, tokens, width)]
    lines.append(jnp.zeros((EXTRA_ROWS - len(lines), width), jnp.float32))
    first_ref[half:] = jnp.concatenate(lines, axis=0).astype(jnp.bfloat16)


def mix(residual, received, row_of, gain):
    tokens, width = residual.shape
    half = tokens // 2
    return pl.pallas_call(
        mix_kernel,
        out_shape=[
            jax.ShapeDtypeStruct((half + EXTRA_ROWS, width), jnp.bfloat16),
            jax.ShapeDtypeStruct((half, width), jnp.bfloat16),
        ],
        in_specs=[pl.BlockSpec(memory_space=pltpu.VMEM)] * 4,
        out_specs=[pl.BlockSpec(memory_space=pltpu.VMEM)] * 2,
        compiler_params=pltpu.CompilerParams(vmem_limit_bytes=40 * 1024 * 1024),
        name="mix",
    )(residual, received, row_of[None, :], gain[None, :])


def scale_kernel(first_ref, second_ref, squares_ref, out_ref):
    half, width = first_ref.shape[0], squares_ref.shape[1]
    lines = out_ref.shape[0] // width
    columns = []
    for i in range(lines):
        line = squares_ref[i : i + 1] + squares_ref[lines + i : lines + i + 1]
        columns.append(jnp.broadcast_to(line, (128, width)).T[:, 0:1])
    inverse = lax.rsqrt(jnp.concatenate(columns, axis=0) / D + 1e-05)
    out_ref[:half] = (first_ref[...] * inverse[:half]).astype(jnp.bfloat16)
    out_ref[half:] = (second_ref[...] * inverse[half:]).astype(jnp.bfloat16)


def scale(first, second, squares):
    return pl.pallas_call(
        scale_kernel,
        out_shape=jax.ShapeDtypeStruct((first.shape[0] + second.shape[0], first.shape[1]), jnp.bfloat16),
        in_specs=[pl.BlockSpec(memory_space=pltpu.VMEM)] * 3,
        out_specs=pl.BlockSpec(memory_space=pltpu.VMEM),
        compiler_params=pltpu.CompilerParams(vmem_limit_bytes=40 * 1024 * 1024),
        name="scale",
    )(first, second, squares)


def ring_projection(halves, full_projection, axis, n):
    me = lax.axis_index(axis)
    rows, width = halves[1].shape
    onward = [(i, (i + 1) % n) for i in range(n)]
    back = [(i, (i - 1) % n) for i in range(n)]

    def product(source, block):
        part = lax.dynamic_slice_in_dim(full_projection, lax.rem(source, n) * width, width, 0)
        return jnp.dot(block[:rows], part, preferred_element_type=jnp.float32)

    arrived = [[(me, block)] for block in halves]
    moving = [[block, block] for block in halves]
    totals = [None, None]
    squares = [halves[0][rows:]]
    for k in range(1, n // 2 + 1):
        for c in range(2):
            if k < n // 2:
                moved = [
                    (me + n - k, lax.ppermute(moving[c][0], axis, onward)),
                    (me + k, lax.ppermute(moving[c][1], axis, back)),
                ]
            elif c == 0:
                moved = [(me + k, lax.ppermute(moving[c][0], axis, onward))]
            else:
                moved = [(me + k, lax.ppermute(moving[c][1], axis, back))]
            for source, block in arrived[c]:
                part = product(source, block)
                totals[c] = part if totals[c] is None else totals[c] + part
            blocks, totals[c] = lax.optimization_barrier(([block for _, block in moved], totals[c]))
            arrived[c] = [(source, block) for (source, _), block in zip(moved, blocks)]
            moving[c] = blocks
            if c == 0:
                squares += [block[rows:] for block in blocks]
    for c in range(2):
        for source, block in arrived[c]:
            totals[c] = totals[c] + product(source, block)
    return totals, sum(part.astype(jnp.float32) for part in squares)


def shards(
    picked_rows,
    w_gate,
    w_up,
    w_down,
    combine_gate,
    pick_owner,
    pick_row,
    residual_in,
    norm_gain,
    projection,
    n_tensor,
):
    my_rows = picked_rows[0]
    capacity = my_rows.shape[0]
    n_groups = pick_owner.shape[0]
    slot_most = max(3 * capacity // n_groups, 2)
    width = residual_in.shape[1]
    my_index = lax.axis_index("expert")

    copies = jnp.broadcast_to(projection[None], (n_groups, *projection.shape))
    full_projection = lax.all_to_all(copies, "expert", split_axis=0, concat_axis=0, tiled=True)
    full_projection = full_projection.reshape(n_groups * projection.shape[0], projection.shape[1])
    parts = gate_up(my_rows, w_gate[0], w_up[0])

    pick_ids = jnp.arange(capacity, dtype=jnp.int32)

    mine = pick_owner == my_index
    before = (pick_ids[:, None] < pick_ids[None, :]).astype(jnp.bfloat16)
    position = jnp.dot(
        mine.astype(jnp.bfloat16), before, preferred_element_type=jnp.float32
    ).astype(jnp.int32)
    slot_range = jnp.arange(slot_most, dtype=jnp.int32)
    matches = mine[:, None, :] & (position[:, None, :] == slot_range[None, :, None])
    row_of = jnp.sum(jnp.where(matches, pick_row[:, None, :] + 1, 0), axis=2) - 1

    sums = lax.psum(tuple(parts), "tensor")
    first, full_projection = lax.optimization_barrier((sums[0], full_projection))
    sums = (first, *sums[1:])
    outgoing = expert_tail(sums, w_down[0], combine_gate[0], pick_owner, n_groups * slot_most)
    outgoing = outgoing.reshape(n_groups, slot_most, width)
    received = lax.all_to_all(outgoing, "expert", split_axis=0, concat_axis=0, tiled=True)
    halves = mix(
        residual_in, received.reshape(n_groups * slot_most, width), row_of.reshape(-1), norm_gain
    )
    totals, squares = ring_projection(halves, full_projection, "tensor", n_tensor)
    return scale(*totals, squares)


def solution(mesh):
    return jax.shard_map(
        functools.partial(shards, n_tensor=mesh.shape["tensor"]),
        mesh=mesh,
        in_specs=(
            P("expert", None, "tensor"),
            P("expert", "tensor", None),
            P("expert", "tensor", None),
            P("expert", None, "tensor"),
            P("expert", None),
            P(),
            P(),
            P("expert", "tensor"),
            P("tensor"),
            P("expert", "tensor"),
        ),
        out_specs=P("expert", "tensor"),
        check_vma=False,
    )
```

```python
import jax
import jax.numpy as jnp
from jax import lax
from jax.experimental import pallas as pl
from jax.experimental.pallas import tpu as pltpu
from jax.sharding import PartitionSpec as P

D = 6144
PART_TYPE = jnp.bfloat16
VMEM_BYTES = 63 * 1024 * 1024
TAIL_BYTES = 49152 * 1024
SPARES = 33
CHUNKS = 1
PART_ROWS = 16


def gate_up_kernel(rows_hbm, gate_hbm, up_hbm, *refs):
    spare_ref, rows_ref, mats_ref, parts_ref, in_sems, out_sems, spare_sems = refs[-7:]
    n_parts = len(refs) - 7 - SPARES
    out_refs, spare_hbms = refs[:n_parts], refs[n_parts:-7]
    capacity, ff = rows_hbm.shape[0], gate_hbm.shape[1]
    cols = ff // CHUNKS
    spare_ref[...] = jnp.zeros_like(spare_ref)
    get_rows = pltpu.make_async_copy(rows_hbm, rows_ref, in_sems.at[2 * CHUNKS])
    get_rows.start()
    gets = []
    for half, mat in enumerate((gate_hbm, up_hbm)):
        for c in range(CHUNKS):
            span = slice(c * cols, (c + 1) * cols)
            gets.append(
                pltpu.make_async_copy(
                    mat.at[:, span], mats_ref.at[half, :, span], in_sems.at[half * CHUNKS + c]
                )
            )
            gets[-1].start()
    spare_puts = [
        pltpu.make_async_copy(spare_ref, spare_hbm, spare_sems.at[n]) for n, spare_hbm in enumerate(spare_hbms)
    ]
    get_rows.wait()
    puts = []
    for half in range(2):
        for c in range(CHUNKS):
            span = slice(c * cols, (c + 1) * cols)
            gets[half * CHUNKS + c].wait()
            parts_ref[half * capacity : (half + 1) * capacity, span] = jnp.dot(
                rows_ref[...], mats_ref[half, :, span], preferred_element_type=jnp.float32
            ).astype(parts_ref.dtype)
        for n in range(half * n_parts // 2, (half + 1) * n_parts // 2):
            puts.append(
                pltpu.make_async_copy(
                    parts_ref.at[n * PART_ROWS : (n + 1) * PART_ROWS], out_refs[n], out_sems.at[n]
                )
            )
            puts[-1].start()
    for put in spare_puts:
        put.start()
    for put in spare_puts + puts:
        put.wait()


def gate_up(rows, gate_mat, up_mat):
    capacity, depth = rows.shape
    ff = gate_mat.shape[1]
    n_parts = 2 * capacity // PART_ROWS
    return pl.pallas_call(
        gate_up_kernel,
        out_shape=[pltpu.HBM((PART_ROWS, ff), PART_TYPE)] * n_parts
        + [pltpu.HBM((16, 128), PART_TYPE)] * SPARES,
        in_specs=[pl.BlockSpec(memory_space=pltpu.HBM)] * 3,
        out_specs=[pl.BlockSpec(memory_space=pltpu.HBM)] * (n_parts + SPARES),
        scratch_shapes=[
            pltpu.VMEM((16, 128), PART_TYPE),
            pltpu.VMEM((capacity, depth), rows.dtype),
            pltpu.VMEM((2, depth, ff), gate_mat.dtype),
            pltpu.VMEM((2 * capacity, ff), PART_TYPE),
            pltpu.SemaphoreType.DMA((2 * CHUNKS + 1,)),
            pltpu.SemaphoreType.DMA((n_parts,)),
            pltpu.SemaphoreType.DMA((SPARES,)),
        ],
        compiler_params=pltpu.CompilerParams(vmem_limit_bytes=VMEM_BYTES),
        name="gate_up",
    )(rows, gate_mat, up_mat)


def tail_kernel(down_ref, combine_ref, owner_ref, *refs):
    out_ref, hidden_ref = refs[-2:]
    capacity = hidden_ref.shape[0]
    half = capacity // PART_ROWS
    sum_refs = refs[: 2 * half]
    slots = out_ref.shape[0]
    owners = owner_ref[pl.ds(lax.axis_index("expert"), 1)].astype(jnp.float32)
    owner_column = jnp.broadcast_to(owners, (128, capacity)).T[:, 0:1]
    pick_row = lax.broadcasted_iota(jnp.int32, (capacity, capacity), 0)
    pick_column = lax.broadcasted_iota(jnp.int32, (capacity, capacity), 1)
    earlier = (owner_column == owners) & (pick_row < pick_column)
    position = jnp.sum(jnp.where(earlier, 1.0, 0.0), axis=0, keepdims=True)
    slot = (owners * (slots // owner_ref.shape[0]) + position).astype(jnp.int32)
    for c in range(half):
        start = c * PART_ROWS
        gate = sum_refs[c][...].astype(jnp.float32)
        up = sum_refs[half + c][...].astype(jnp.float32)
        hidden_ref[start : start + PART_ROWS] = (gate / (1.0 + jnp.exp(-gate)) * up).astype(jnp.bfloat16)
    expert_out = jnp.dot(hidden_ref[...], down_ref[...], preferred_element_type=jnp.float32)
    combine = jnp.broadcast_to(combine_ref[...], (128, capacity)).T[:, 0:1]
    weighted = (combine * expert_out).astype(jnp.bfloat16)
    slot_ids = lax.broadcasted_iota(jnp.int32, (slots, capacity), 0)
    table = jnp.where(slot == slot_ids, 1.0, 0.0).astype(jnp.bfloat16)
    out_ref[...] = jnp.dot(table, weighted, preferred_element_type=jnp.float32).astype(jnp.bfloat16)


def expert_tail(sums, down_mat, combine, pick_owner, slots):
    ff, width = down_mat.shape
    capacity = combine.shape[0]
    n_parts = 2 * capacity // PART_ROWS
    return pl.pallas_call(
        tail_kernel,
        out_shape=jax.ShapeDtypeStruct((slots, width), jnp.bfloat16),
        in_specs=[pl.BlockSpec(memory_space=pltpu.VMEM)] * (3 + n_parts)
        + [pl.BlockSpec(memory_space=pl.ANY)] * (len(sums) - n_parts),
        out_specs=pl.BlockSpec(memory_space=pltpu.VMEM),
        scratch_shapes=[
            pltpu.VMEM((capacity, ff), jnp.bfloat16),
        ],
        compiler_params=pltpu.CompilerParams(vmem_limit_bytes=TAIL_BYTES),
        name="expert_tail",
    )(down_mat, combine[None, :], pick_owner, *sums)


def mix_kernel(residual_ref, received_ref, row_ref, gain_ref, out_ref, squares_ref):
    tokens, width = residual_ref.shape
    slots = received_ref.shape[0]
    token_ids = lax.broadcasted_iota(jnp.int32, (tokens, slots), 0)
    table = jnp.where(row_ref[...] == token_ids, 1.0, 0.0).astype(jnp.bfloat16)
    moe = jnp.dot(table, received_ref[...], preferred_element_type=jnp.float32)
    mixed = residual_ref[...].astype(jnp.float32) + moe
    out_ref[...] = (mixed * gain_ref[...]).astype(jnp.bfloat16)
    squares = jnp.sum(mixed * mixed, axis=1, keepdims=True)
    squares_ref[...] = jnp.broadcast_to(squares, (tokens, 128)).T[0:1]


def mix(residual, received, row_of, gain):
    tokens, width = residual.shape
    return pl.pallas_call(
        mix_kernel,
        out_shape=[
            jax.ShapeDtypeStruct((tokens, width), jnp.bfloat16),
            jax.ShapeDtypeStruct((1, tokens), jnp.float32),
        ],
        in_specs=[pl.BlockSpec(memory_space=pltpu.VMEM)] * 4,
        out_specs=[pl.BlockSpec(memory_space=pltpu.VMEM)] * 2,
        compiler_params=pltpu.CompilerParams(vmem_limit_bytes=40 * 1024 * 1024),
        name="mix",
    )(residual, received, row_of[None, :], gain[None, :])


def final_kernel(gathered_ref, proj_ref, squares_ref, out_ref, acc_ref):
    step = pl.program_id(0)
    per_step, tokens, width = gathered_ref.shape
    block = jnp.concatenate([gathered_ref[z] for z in range(per_step)], axis=1)
    total = jnp.dot(block, proj_ref[...], preferred_element_type=jnp.float32)

    @pl.when(step == 0)
    def _():
        acc_ref[...] = total

    @pl.when(step > 0)
    def _():
        acc_ref[...] += total

    @pl.when(step == pl.num_programs(0) - 1)
    def _():
        inverse = lax.rsqrt(squares_ref[...] / D + 1e-05)
        column = jnp.broadcast_to(inverse, (128, tokens)).T[:, 0:1]
        out_ref[...] = (acc_ref[...] * column).astype(jnp.bfloat16)


def final(gathered, full_projection, square_total):
    n, tokens, width = gathered.shape
    columns = full_projection.shape[1]
    per_step = 8
    return pl.pallas_call(
        final_kernel,
        grid=(n // per_step,),
        out_shape=jax.ShapeDtypeStruct((tokens, columns), jnp.bfloat16),
        in_specs=[
            pl.BlockSpec((per_step, tokens, width), lambda i: (i, 0, 0)),
            pl.BlockSpec((per_step * width, columns), lambda i: (i, 0)),
            pl.BlockSpec((1, tokens), lambda i: (0, 0)),
        ],
        out_specs=pl.BlockSpec((tokens, columns), lambda i: (0, 0)),
        scratch_shapes=[pltpu.VMEM((tokens, columns), jnp.float32)],
        compiler_params=pltpu.CompilerParams(vmem_limit_bytes=VMEM_BYTES),
        name="final",
    )(gathered, full_projection, square_total)


def shards(
    picked_rows,
    w_gate,
    w_up,
    w_down,
    combine_gate,
    pick_owner,
    pick_row,
    residual_in,
    norm_gain,
    projection,
):
    my_rows = picked_rows[0]
    capacity = my_rows.shape[0]
    n_groups = pick_owner.shape[0]
    slot_most = max(3 * capacity // n_groups, 2)
    width = residual_in.shape[1]
    my_index = lax.axis_index("expert")

    parts = gate_up(my_rows, w_gate[0], w_up[0])

    pick_ids = jnp.arange(capacity, dtype=jnp.int32)

    mine = pick_owner == my_index
    before = (pick_ids[:, None] < pick_ids[None, :]).astype(jnp.bfloat16)
    position = jnp.dot(
        mine.astype(jnp.bfloat16), before, preferred_element_type=jnp.float32
    ).astype(jnp.int32)
    slot_range = jnp.arange(slot_most, dtype=jnp.int32)
    matches = mine[:, None, :] & (position[:, None, :] == slot_range[None, :, None])
    row_of = jnp.sum(jnp.where(matches, pick_row[:, None, :] + 1, 0), axis=2) - 1

    sums = lax.psum(tuple(parts), "tensor")
    outgoing = expert_tail(sums, w_down[0], combine_gate[0], pick_owner, n_groups * slot_most)
    outgoing = outgoing.reshape(n_groups, slot_most, width)
    received = lax.all_to_all(outgoing, "expert", split_axis=0, concat_axis=0, tiled=True)
    gained, squares = mix(
        residual_in, received.reshape(n_groups * slot_most, width), row_of.reshape(-1), norm_gain
    )
    full_gained = lax.all_gather(gained, "tensor")
    square_total = lax.psum(squares, "tensor")
    square_total, projection = lax.optimization_barrier((square_total, projection))
    copies = jnp.broadcast_to(projection[None], (n_groups, *projection.shape))
    full_projection = lax.all_to_all(copies, "expert", split_axis=0, concat_axis=0, tiled=True)
    full_projection = full_projection.reshape(n_groups * projection.shape[0], width)
    return final(full_gained, full_projection, square_total)


def solution(mesh):
    return jax.shard_map(
        shards,
        mesh=mesh,
        in_specs=(
            P("expert", None, "tensor"),
            P("expert", "tensor", None),
            P("expert", "tensor", None),
            P("expert", None, "tensor"),
            P("expert", None),
            P(),
            P(),
            P("expert", "tensor"),
            P("tensor"),
            P("expert", "tensor"),
        ),
        out_specs=P("expert", "tensor"),
        check_vma=False,
    )
```

```python
import jax
import jax.numpy as jnp
from jax import lax
from jax.experimental import pallas as pl
from jax.experimental.pallas import tpu as pltpu
from jax.sharding import PartitionSpec as P

D = 6144
PART_TYPE = jnp.bfloat16
VMEM_BYTES = 63 * 1024 * 1024
TAIL_BYTES = 49152 * 1024
SPARES = 33
CHUNKS = 1
PART_ROWS = 16


def gate_up_kernel(rows_hbm, gate_hbm, up_hbm, *refs):
    spare_ref, rows_ref, mats_ref, parts_ref, in_sems, out_sems, spare_sems = refs[-7:]
    n_parts = len(refs) - 7 - SPARES
    out_refs, spare_hbms = refs[:n_parts], refs[n_parts:-7]
    capacity, ff = rows_hbm.shape[0], gate_hbm.shape[1]
    cols = ff // CHUNKS
    spare_ref[...] = jnp.zeros_like(spare_ref)
    get_rows = pltpu.make_async_copy(rows_hbm, rows_ref, in_sems.at[2 * CHUNKS])
    get_rows.start()
    gets = []
    for half, mat in enumerate((gate_hbm, up_hbm)):
        for c in range(CHUNKS):
            span = slice(c * cols, (c + 1) * cols)
            gets.append(
                pltpu.make_async_copy(
                    mat.at[:, span], mats_ref.at[half, :, span], in_sems.at[half * CHUNKS + c]
                )
            )
            gets[-1].start()
    spare_puts = [
        pltpu.make_async_copy(spare_ref, spare_hbm, spare_sems.at[n]) for n, spare_hbm in enumerate(spare_hbms)
    ]
    get_rows.wait()
    puts = []
    for half in range(2):
        for c in range(CHUNKS):
            span = slice(c * cols, (c + 1) * cols)
            gets[half * CHUNKS + c].wait()
            parts_ref[half * capacity : (half + 1) * capacity, span] = jnp.dot(
                rows_ref[...], mats_ref[half, :, span], preferred_element_type=jnp.float32
            ).astype(parts_ref.dtype)
        for n in range(half * n_parts // 2, (half + 1) * n_parts // 2):
            puts.append(
                pltpu.make_async_copy(
                    parts_ref.at[n * PART_ROWS : (n + 1) * PART_ROWS], out_refs[n], out_sems.at[n]
                )
            )
            puts[-1].start()
    for put in spare_puts:
        put.start()
    for put in spare_puts + puts:
        put.wait()


def gate_up(rows, gate_mat, up_mat):
    capacity, depth = rows.shape
    ff = gate_mat.shape[1]
    n_parts = 2 * capacity // PART_ROWS
    return pl.pallas_call(
        gate_up_kernel,
        out_shape=[pltpu.HBM((PART_ROWS, ff), PART_TYPE)] * n_parts
        + [pltpu.HBM((16, 128), PART_TYPE)] * SPARES,
        in_specs=[pl.BlockSpec(memory_space=pltpu.HBM)] * 3,
        out_specs=[pl.BlockSpec(memory_space=pltpu.HBM)] * (n_parts + SPARES),
        scratch_shapes=[
            pltpu.VMEM((16, 128), PART_TYPE),
            pltpu.VMEM((capacity, depth), rows.dtype),
            pltpu.VMEM((2, depth, ff), gate_mat.dtype),
            pltpu.VMEM((2 * capacity, ff), PART_TYPE),
            pltpu.SemaphoreType.DMA((2 * CHUNKS + 1,)),
            pltpu.SemaphoreType.DMA((n_parts,)),
            pltpu.SemaphoreType.DMA((SPARES,)),
        ],
        compiler_params=pltpu.CompilerParams(vmem_limit_bytes=VMEM_BYTES),
        name="gate_up",
    )(rows, gate_mat, up_mat)


def tail_kernel(down_ref, picks_ref, *refs):
    out_ref, hidden_ref = refs[-2:]
    capacity = hidden_ref.shape[0]
    half = capacity // PART_ROWS
    sum_refs = refs[: 2 * half]
    slots = out_ref.shape[0]
    owners = picks_ref[pl.ds(lax.axis_index("expert") + 1, 1)]
    owner_column = jnp.broadcast_to(owners, (128, capacity)).T[:, 0:1]
    pick_row = lax.broadcasted_iota(jnp.int32, (capacity, capacity), 0)
    pick_column = lax.broadcasted_iota(jnp.int32, (capacity, capacity), 1)
    earlier = (owner_column == owners) & (pick_row < pick_column)
    position = jnp.sum(jnp.where(earlier, 1.0, 0.0), axis=0, keepdims=True)
    slot = (owners * (slots // (picks_ref.shape[0] - 1)) + position).astype(jnp.int32)
    for c in range(half):
        start = c * PART_ROWS
        gate = sum_refs[c][...].astype(jnp.float32)
        up = sum_refs[half + c][...].astype(jnp.float32)
        hidden_ref[start : start + PART_ROWS] = (gate / (1.0 + jnp.exp(-gate)) * up).astype(jnp.bfloat16)
    expert_out = jnp.dot(hidden_ref[...], down_ref[...], preferred_element_type=jnp.float32)
    combine = jnp.broadcast_to(picks_ref[0:1], (128, capacity)).T[:, 0:1]
    weighted = (combine * expert_out).astype(jnp.bfloat16)
    slot_ids = lax.broadcasted_iota(jnp.int32, (slots, capacity), 0)
    table = jnp.where(slot == slot_ids, 1.0, 0.0).astype(jnp.bfloat16)
    out_ref[...] = jnp.dot(table, weighted, preferred_element_type=jnp.float32).astype(jnp.bfloat16)


def expert_tail(sums, down_mat, combine, pick_owner, slots):
    ff, width = down_mat.shape
    capacity = combine.shape[0]
    n_parts = 2 * capacity // PART_ROWS
    picks = jnp.concatenate([combine[None, :], pick_owner.astype(jnp.float32)], axis=0)
    return pl.pallas_call(
        tail_kernel,
        out_shape=jax.ShapeDtypeStruct((slots, width), jnp.bfloat16),
        in_specs=[pl.BlockSpec(memory_space=pltpu.VMEM)] * (2 + n_parts)
        + [pl.BlockSpec(memory_space=pl.ANY)] * (len(sums) - n_parts),
        out_specs=pl.BlockSpec(memory_space=pltpu.VMEM),
        scratch_shapes=[
            pltpu.VMEM((capacity, ff), jnp.bfloat16),
        ],
        compiler_params=pltpu.CompilerParams(vmem_limit_bytes=TAIL_BYTES),
        name="expert_tail",
    )(down_mat, picks, *sums)


def mix_kernel(residual_ref, received_ref, row_ref, gain_ref, out_ref, squares_ref):
    tokens, width = residual_ref.shape
    slots = received_ref.shape[0]
    token_ids = lax.broadcasted_iota(jnp.int32, (tokens, slots), 0)
    table = jnp.where(row_ref[...] == token_ids, 1.0, 0.0).astype(jnp.bfloat16)
    moe = jnp.dot(table, received_ref[...], preferred_element_type=jnp.float32)
    mixed = residual_ref[...].astype(jnp.float32) + moe
    out_ref[...] = (mixed * gain_ref[...]).astype(jnp.bfloat16)
    squares = jnp.sum(mixed * mixed, axis=1, keepdims=True)
    squares_ref[...] = jnp.broadcast_to(squares, (tokens, 128)).T[0:1]


def mix(residual, received, row_of, gain):
    tokens, width = residual.shape
    return pl.pallas_call(
        mix_kernel,
        out_shape=[
            jax.ShapeDtypeStruct((tokens, width), jnp.bfloat16),
            jax.ShapeDtypeStruct((1, tokens), jnp.float32),
        ],
        in_specs=[pl.BlockSpec(memory_space=pltpu.VMEM)] * 4,
        out_specs=[pl.BlockSpec(memory_space=pltpu.VMEM)] * 2,
        compiler_params=pltpu.CompilerParams(vmem_limit_bytes=40 * 1024 * 1024),
        name="mix",
    )(residual, received, row_of[None, :], gain[None, :])


def final_kernel(gathered_ref, proj_ref, squares_ref, out_ref, acc_ref):
    step = pl.program_id(0)
    per_step, tokens, width = gathered_ref.shape
    block = jnp.concatenate([gathered_ref[z] for z in range(per_step)], axis=1)
    total = jnp.dot(block, proj_ref[...], preferred_element_type=jnp.float32)

    @pl.when(step == 0)
    def _():
        acc_ref[...] = total

    @pl.when(step > 0)
    def _():
        acc_ref[...] += total

    @pl.when(step == pl.num_programs(0) - 1)
    def _():
        inverse = lax.rsqrt(squares_ref[...] / D + 1e-05)
        column = jnp.broadcast_to(inverse, (128, tokens)).T[:, 0:1]
        out_ref[...] = (acc_ref[...] * column).astype(jnp.bfloat16)


def final(gathered, full_projection, square_total):
    n, tokens, width = gathered.shape
    columns = full_projection.shape[1]
    per_step = 8
    return pl.pallas_call(
        final_kernel,
        grid=(n // per_step,),
        out_shape=jax.ShapeDtypeStruct((tokens, columns), jnp.bfloat16),
        in_specs=[
            pl.BlockSpec((per_step, tokens, width), lambda i: (i, 0, 0)),
            pl.BlockSpec((per_step * width, columns), lambda i: (i, 0)),
            pl.BlockSpec((1, tokens), lambda i: (0, 0)),
        ],
        out_specs=pl.BlockSpec((tokens, columns), lambda i: (0, 0)),
        scratch_shapes=[pltpu.VMEM((tokens, columns), jnp.float32)],
        compiler_params=pltpu.CompilerParams(vmem_limit_bytes=VMEM_BYTES),
        name="final",
    )(gathered, full_projection, square_total)


def shards(
    picked_rows,
    w_gate,
    w_up,
    w_down,
    combine_gate,
    pick_owner,
    pick_row,
    residual_in,
    norm_gain,
    projection,
):
    my_rows = picked_rows[0]
    capacity = my_rows.shape[0]
    n_groups = pick_owner.shape[0]
    slot_most = max(3 * capacity // n_groups, 2)
    width = residual_in.shape[1]
    my_index = lax.axis_index("expert")

    parts = gate_up(my_rows, w_gate[0], w_up[0])

    pick_ids = jnp.arange(capacity, dtype=jnp.int32)

    mine = pick_owner == my_index
    before = (pick_ids[:, None] < pick_ids[None, :]).astype(jnp.bfloat16)
    position = jnp.dot(
        mine.astype(jnp.bfloat16), before, preferred_element_type=jnp.float32
    ).astype(jnp.int32)
    slot_range = jnp.arange(slot_most, dtype=jnp.int32)
    matches = mine[:, None, :] & (position[:, None, :] == slot_range[None, :, None])
    row_of = jnp.sum(jnp.where(matches, pick_row[:, None, :] + 1, 0), axis=2) - 1

    sums = lax.psum(tuple(parts), "tensor")
    outgoing = expert_tail(sums, w_down[0], combine_gate[0], pick_owner, n_groups * slot_most)
    outgoing = outgoing.reshape(n_groups, slot_most, width)
    received = lax.all_to_all(outgoing, "expert", split_axis=0, concat_axis=0, tiled=True)
    gained, squares = mix(
        residual_in, received.reshape(n_groups * slot_most, width), row_of.reshape(-1), norm_gain
    )
    full_gained = lax.all_gather(gained, "tensor")
    square_total = lax.psum(squares, "tensor")
    square_total, projection = lax.optimization_barrier((square_total, projection))
    copies = jnp.broadcast_to(projection[None], (n_groups, *projection.shape))
    full_projection = lax.all_to_all(copies, "expert", split_axis=0, concat_axis=0, tiled=True)
    full_projection = full_projection.reshape(n_groups * projection.shape[0], width)
    return final(full_gained, full_projection, square_total)


def solution(mesh):
    return jax.shard_map(
        shards,
        mesh=mesh,
        in_specs=(
            P("expert", None, "tensor"),
            P("expert", "tensor", None),
            P("expert", "tensor", None),
            P("expert", None, "tensor"),
            P("expert", None),
            P(),
            P(),
            P("expert", "tensor"),
            P("tensor"),
            P("expert", "tensor"),
        ),
        out_specs=P("expert", "tensor"),
        check_vma=False,
    )
```
